256 devices in a mesh: sky: 64 (over z, y, core), batch: 4 (over x).
Axes of the slice: x: 4, y: 4, z: 8, core: 2. Of those that a mesh axis runs over, the one named last changes fastest.
Arguments:
- features: float32 [4, 64, 80, 1024], P('batch', 'sky'), may hold values from -0.1875 to 0.1875
- target: float32 [4, 64, 576, 1024], P('batch', 'sky'), may hold values from -2 to 2
- images: float32 [4, 64, 16, 80], P('batch', 'sky'), may hold values from -6 to 6
- layer_mask: int32 [4, 64, 16], P('batch', 'sky'), may hold values 0 or 1
- pair_list: int32 [4, 64, 9], P('batch', 'sky'), may hold values from 0 to 11, as said below
- ridge_weight: float32 [4, 64], P('batch', 'sky'), may hold values from 0.2 to 1
Outputs:
- transfer: float32 [4, 64, 720, 576], P('batch', 'sky')
- final_image: float32 [16, 96, 1536], P(None, 'batch', 'sky')
The draws below stay inside these ranges and needn't reach their ends.
Inputs may be any that keep to these rules, and one draw needn't show every extreme that they name: `pair_list`: the 9 entries of each output stamp are distinct candidate numbers.
All inputs are finite; a program needn't handle non-finite values. No bound on the sum of `layer_mask` on one device may be relied on, other than what follows from the above.
Results may differ from the reference program's by a relative error of at most 0.0003.
Values sent between devices are 32-bit elements; how exact they have to be, the bound alone decides.
A program may use at most 128 MiB of HBM per device.

```python
import math
import jax
import jax.numpy as jnp
from jax import lax

NPIX = 80
FEAT = 1024
SIDE = 24
LAYERS = 16
NSEL = 9
FADE = 4
ORDER = 720
NOUT_PIX = 576
CAND = 12
N_SKY = 64
N_BATCH = 4


def draw_pair_list(key, part):
    scores = jax.random.randint(key, (N_BATCH, N_SKY, CAND), 0, 65536) * CAND + jnp.arange(CAND, dtype=jnp.int32)
    ordering = jnp.argsort(scores, axis=-1, stable=True)
    return ordering[..., :NSEL].astype(jnp.int32)


def plant(array, stream_key, smallest, top_value):
    extent = array.shape
    spot = [jax.random.randint(jax.random.fold_in(stream_key, axis), (), 0, extent[axis]) for axis in range(len(extent))]
    array = array.at[tuple(spot)].set(smallest)
    longest = extent.index(max(extent))
    spot[longest] = (spot[longest] + 1) % extent[longest]
    return array.at[tuple(spot)].set(top_value)


def level_of(own_key, shape, split, smallest, top_value):
    def one(axis_at, blocks):
        steps = jax.random.uniform(jax.random.fold_in(jax.random.fold_in(own_key, 6), axis_at), (blocks,), jnp.float32, smallest / len(split), top_value / len(split))
        return jnp.repeat(jnp.exp(steps), shape[axis_at] // blocks).reshape((-1,) + (1,) * (len(shape) - axis_at - 1))

    gain = one(*split[0])
    for cut in split[1:]:
        gain = gain * one(*cut)
    return gain


def noise(rng, shape, scale, most, pieces=(), kind=jnp.bfloat16):
    loudness = level_of(rng, shape, pieces, -0.22, 0.18) if pieces else 1.0
    result = jax.random.normal(rng, shape, jnp.float32) * scale * loudness
    return jnp.minimum(jnp.maximum(result, -most), most).astype(kind)


def setup_inputs(seed: int = 0) -> dict:
    splits = jax.random.split(jax.random.key(seed), 7)
    features = noise(splits[0], (N_BATCH, N_SKY, NPIX, FEAT), FEAT ** -0.5, 0.1875, ((0, 4), (1, 64)), jnp.float32)
    target = noise(splits[1], (N_BATCH, N_SKY, NOUT_PIX, FEAT), 0.15, 2.0, ((0, 4), (1, 64)), jnp.float32)
    images = noise(splits[2], (N_BATCH, N_SKY, LAYERS, NPIX), 1.0, 6.0, ((0, 4), (1, 64)), jnp.float32)
    layer_mask = plant((jax.random.randint(splits[3], (N_BATCH, N_SKY, LAYERS), 0, 4) < 3).astype(jnp.int32), jax.random.fold_in(splits[3], 1), 0, 1)
    pair_list = draw_pair_list(jax.random.fold_in(splits[6], 71), 0)
    ridge_weight = jnp.clip(jnp.exp(math.log(1.0) - 1.609438 * jax.random.uniform(splits[5], (N_BATCH, N_SKY), jnp.float32) ** level_of(splits[5], (N_BATCH, N_SKY), ((0, 4), (1, 64)), -0.2, 0.2)), 0.2, 1.0)
    return {"features": features, "target": target, "images": images, "layer_mask": layer_mask, "pair_list": pair_list, "ridge_weight": ridge_weight}


precise = lax.Precision.HIGHEST

def reference(features, target, images, layer_mask, pair_list, ridge_weight):
    masked = images * layer_mask[..., None].astype(jnp.float32)
    padded_feat = jnp.pad(features, ((0, 0), (1, 1), (0, 0), (0, 0)))
    padded_image = jnp.pad(masked, ((0, 0), (1, 1), (0, 0), (0, 0)))

    def per_stamp(flat_index):
        batch_pos = flat_index // N_SKY
        sky_pos = flat_index % N_SKY
        window = lax.dynamic_slice_in_dim(padded_feat, sky_pos, 3, 1).reshape(CAND, NPIX, FEAT)
        image_window = lax.dynamic_slice_in_dim(padded_image, sky_pos, 3, 1).reshape(CAND, LAYERS, NPIX)
        chosen = pair_list[batch_pos, sky_pos]
        chosen_feat = window[chosen].reshape(ORDER, FEAT)
        chosen_image = image_window[chosen]
        system = jnp.dot(chosen_feat, chosen_feat.T, precision=precise)
        system = system + ridge_weight[batch_pos, sky_pos] * jnp.eye(ORDER, dtype=jnp.float32)
        right_sides = jnp.dot(chosen_feat, target[batch_pos, sky_pos].T, precision=precise)
        factor = jnp.linalg.cholesky(system)
        midway = lax.linalg.triangular_solve(factor, right_sides, left_side=True, lower=True)
        transfer = lax.linalg.triangular_solve(factor, midway, left_side=True, lower=True, transpose_a=True)
        coadded = jnp.einsum('kio,kli->lo', transfer.reshape(NSEL, NPIX, NOUT_PIX), chosen_image, precision=precise)
        return (transfer, coadded.reshape(LAYERS, SIDE, SIDE))
    transfer_all, coadded_all = lax.map(per_stamp, jnp.arange(N_BATCH * N_SKY, dtype=jnp.int32))
    transfer_all = transfer_all.reshape(N_BATCH, N_SKY, ORDER, NOUT_PIX)
    stamps_grid = coadded_all.reshape(N_BATCH, N_SKY, LAYERS, SIDE, SIDE)
    padded_grid = jnp.pad(stamps_grid, ((1, 1), (1, 1), (0, 0), (0, 0), (0, 0)))
    east_strip = padded_grid[1:-1, 2:, :, :, :FADE]
    west_strip = padded_grid[1:-1, :-2, :, :, SIDE - FADE:]
    south_strip = padded_grid[2:, 1:-1, :, :FADE, :]
    north_strip = padded_grid[:-2, 1:-1, :, SIDE - FADE:, :]
    fade_ramp = (jnp.arange(FADE, dtype=jnp.float32) + 1.0) / (FADE + 1.0)
    blended = stamps_grid
    blended = blended.at[..., :, SIDE - FADE:].add(fade_ramp * east_strip)
    blended = blended.at[..., :, :FADE].add(fade_ramp[::-1] * west_strip)
    blended = blended.at[..., SIDE - FADE:, :].add(fade_ramp[:, None] * south_strip)
    blended = blended.at[..., :FADE, :].add(fade_ramp[::-1][:, None] * north_strip)
    final_image = blended.transpose(2, 0, 3, 1, 4).reshape(LAYERS, N_BATCH * SIDE, N_SKY * SIDE)
    return (transfer_all, final_image)
```

```python
import functools

import jax
import jax.numpy as jnp
from jax import lax
from jax.experimental import pallas as pl
from jax.experimental.pallas import tpu as pltpu
from jax.sharding import PartitionSpec as P

NPIX = 80
FEAT = 1024
SIDE = 24
LAYERS = 16
NSEL = 9
FADE = 4
ORDER = 720
NOUT_PIX = 576
CAND = 12

TILE = 128
NBLOCK = 6
PADDED = TILE * NBLOCK
HALF = NPIX // 2
MESH = pl.DeviceIdType.MESH
HIGH = lax.Precision.HIGH
F32 = jnp.float32
BF16 = jnp.bfloat16


def gather_kernel(
    n_sky, n_batch, feat_ref, image_ref, mask_ref, window_ref, stamps_ref,
    masked, zeros, zero_image, local_sem, fs_sem, fr_sem, ys_sem, yr_sem, is_sem, ir_sem, js_sem, jr_sem,
):
    s = lax.axis_index("sky")
    b = lax.axis_index("batch")
    up = lax.rem(s + 1, n_sky)
    down = lax.rem(s + n_sky - 1, n_sky)
    right = lax.rem(b + 1, n_batch)
    left = lax.rem(b + n_batch - 1, n_batch)
    far = lax.rem(b + 2, n_batch)

    barrier = pltpu.get_barrier_semaphore()
    for where in ((s, left), (s, right), (up, b), (down, b)):
        pl.semaphore_signal(barrier, inc=1, device_id=where, device_id_type=MESH)

    row = lax.broadcasted_iota(jnp.int32, (LAYERS, NPIX), 0)
    keep = jnp.zeros((LAYERS, NPIX), jnp.int32)
    for layer in range(LAYERS):
        keep = jnp.where(row == layer, mask_ref[layer], keep)
    masked[...] = jnp.zeros((LAYERS, TILE), F32)
    masked[:, :NPIX] = image_ref[...] * keep.astype(F32)
    zeros[...] = jnp.zeros((NPIX, FEAT), F32)
    zero_image[...] = jnp.zeros((LAYERS, TILE), F32)

    pl.semaphore_wait(barrier, 4)

    rows = (pl.ds(0, HALF), pl.ds(HALF, HALF))

    def remote(src, dst, send, recv, where):
        return pltpu.make_async_remote_copy(
            src_ref=src, dst_ref=dst, send_sem=send, recv_sem=recv, device_id=where, device_id_type=MESH
        )

    def along(number, owner, half, where, src=None):
        slot = window_ref.at[3 * owner + 1, rows[half]]
        return remote(slot if src is None else src, slot, fs_sem.at[number], fr_sem.at[number], where)

    own_half = (feat_ref.at[rows[0]], feat_ref.at[rows[1]])
    sends = []
    for half in (0, 1):
        sends += [
            along(0 + half, b, half, (s, right), own_half[half]),
            along(2 + half, b, half, (s, left), own_half[half]),
        ]
        for copy in sends[-2:]:
            copy.start()

    def across(place, owner, half, src=None):
        base = window_ref.at[3 * owner + 1, rows[half]] if src is None else src
        number = 2 * place + half
        return (
            remote(base, window_ref.at[3 * owner, rows[half]], ys_sem.at[0, number], yr_sem.at[0, number], (up, b)),
            remote(base, window_ref.at[3 * owner + 2, rows[half]], ys_sem.at[1, number], yr_sem.at[1, number], (down, b)),
        )

    def start(copies):
        for copy in copies:
            copy.start()
        sends.extend(copies)

    for half in (0, 1):
        start(across(0, b, half, own_half[half]))

    own = [
        pltpu.make_async_copy(feat_ref, window_ref.at[3 * b + 1], local_sem.at[0]),
        pltpu.make_async_copy(masked, stamps_ref.at[3 * b + 1], local_sem.at[1]),
    ]
    for copy in own:
        copy.start()

    def image_along(number, owner, where, src):
        return remote(src, stamps_ref.at[3 * owner + 1], is_sem.at[number], ir_sem.at[number], where)

    def image_across(place, owner, src):
        return (
            remote(src, stamps_ref.at[3 * owner], js_sem.at[0, place], jr_sem.at[0, place], (up, b)),
            remote(src, stamps_ref.at[3 * owner + 2], js_sem.at[1, place], jr_sem.at[1, place], (down, b)),
        )

    start((image_along(0, b, (s, right), masked), image_along(1, b, (s, left), masked)))
    start(image_across(0, b, masked))

    along(0, left, 0, (s, left)).wait_recv()
    start((along(4, left, 0, (s, right)),))
    start(across(1, left, 0))
    along(2, right, 0, (s, right)).wait_recv()
    start(across(2, right, 0))
    along(3, right, 1, (s, right)).wait_recv()
    start((along(5, right, 1, (s, left)),))
    start(across(2, right, 1))
    along(1, left, 1, (s, left)).wait_recv()
    start(across(1, left, 1))

    image_along(0, left, (s, left), stamps_ref.at[3 * left + 1]).wait_recv()
    start((image_along(2, left, (s, right), stamps_ref.at[3 * left + 1]),))
    start(image_across(1, left, stamps_ref.at[3 * left + 1]))
    image_along(1, right, (s, right), stamps_ref.at[3 * right + 1]).wait_recv()
    start(image_across(2, right, stamps_ref.at[3 * right + 1]))
    image_along(2, far, (s, left), stamps_ref.at[3 * far + 1]).wait_recv()
    start(image_across(3, far, stamps_ref.at[3 * far + 1]))

    along(4, far, 0, (s, left)).wait_recv()
    start(across(3, far, 0))
    along(5, far, 1, (s, right)).wait_recv()
    start(across(3, far, 1))

    for place, owner in enumerate((b, left, right, far)):
        for half in (0, 1):
            for copy in across(place, owner, half):
                copy.wait_recv()
        for copy in image_across(place, owner, stamps_ref.at[3 * owner + 1]):
            copy.wait_recv()
    for copy in sends:
        copy.wait_send()
    for copy in own:
        copy.wait()

    def blank(side):
        for owner in range(n_batch):
            copy = pltpu.make_async_copy(zeros, window_ref.at[3 * owner + side], local_sem.at[0])
            other = pltpu.make_async_copy(zero_image, stamps_ref.at[3 * owner + side], local_sem.at[1])
            copy.start()
            other.start()
            copy.wait()
            other.wait()

    @pl.when(s == 0)
    def _():
        blank(0)

    @pl.when(s == n_sky - 1)
    def _():
        blank(2)


def gather_window(features, images, layer_mask):
    n_sky, n_batch = lax.axis_size("sky"), lax.axis_size("batch")
    return pl.pallas_call(
        functools.partial(gather_kernel, n_sky, n_batch),
        out_shape=(
            jax.ShapeDtypeStruct((CAND, NPIX, FEAT), F32),
            jax.ShapeDtypeStruct((CAND, LAYERS, TILE), F32),
        ),
        in_specs=[
            pl.BlockSpec(memory_space=pltpu.VMEM),
            pl.BlockSpec(memory_space=pltpu.VMEM),
            pl.BlockSpec(memory_space=pltpu.SMEM),
        ],
        out_specs=(pl.BlockSpec(memory_space=pl.ANY), pl.BlockSpec(memory_space=pl.ANY)),
        scratch_shapes=[
            pltpu.VMEM((LAYERS, TILE), F32),
            pltpu.VMEM((NPIX, FEAT), F32),
            pltpu.VMEM((LAYERS, TILE), F32),
            pltpu.SemaphoreType.DMA((2,)),
            pltpu.SemaphoreType.DMA((6,)),
            pltpu.SemaphoreType.DMA((6,)),
            pltpu.SemaphoreType.DMA((2, 8)),
            pltpu.SemaphoreType.DMA((2, 8)),
            pltpu.SemaphoreType.DMA((3,)),
            pltpu.SemaphoreType.DMA((3,)),
            pltpu.SemaphoreType.DMA((2, 4)),
            pltpu.SemaphoreType.DMA((2, 4)),
        ],
        compiler_params=pltpu.CompilerParams(collective_id=0, has_side_effects=True),
        name="gather_window",
    )(features, images, layer_mask)


def row_of(tile, index):
    return jnp.broadcast_to(tile[index : index + 1, :], (8, TILE))


def column_of(tile, index):
    return jnp.broadcast_to(tile[:, index : index + 1], (8, TILE))


def total(terms):
    while len(terms) > 1:
        terms = [terms[i] + terms[i + 1] if i + 1 < len(terms) else terms[i] for i in range(0, len(terms), 2)]
    return terms[0]


def invert_small(columns, row):
    columns = list(columns)
    for p in range(8):
        scale = 1.0 / row_of(columns[p], p)
        pivot = columns[p]
        here = row == p
        for j in range(8):
            if j != p:
                scaled = row_of(columns[j], p) * scale
                columns[j] = jnp.where(here, scaled, columns[j] - pivot * scaled)
        columns[p] = jnp.where(here, scale, -pivot * scale)
    return columns


def invert_tile(groups):
    row = lax.broadcasted_iota(jnp.int32, (8, TILE), 0)
    lane = lax.broadcasted_iota(jnp.int32, (8, TILE), 1)
    groups = list(groups)
    count = len(groups)
    for k in range(count):
        inside = (lane >= 8 * k) & (lane < 8 * k + 8)
        small = invert_small([column_of(groups[k], 8 * k + j) for j in range(8)], row)
        panel = jnp.where(inside, jnp.where(lane - 8 * k == row, 1.0, 0.0), groups[k])
        panel = total([small[j] * row_of(panel, j) for j in range(8)])
        rows = [row_of(panel, j) for j in range(8)]
        for step in range(1, count):
            i = (k + step) % count
            change = total([column_of(groups[i], 8 * k + j) * rows[j] for j in range(8)])
            groups[i] = jnp.where(inside, 0.0, groups[i]) - change
        groups[k] = panel
    return groups


def dot(a, b, dims=((1,), (0,))):
    return lax.dot_general(a, b, (dims, ((), ())), precision=HIGH, preferred_element_type=F32)


def halves(x):
    top = x.astype(BF16)
    return top, (x - top.astype(F32)).astype(BF16)


def solve_kernel(
    pair_ref, ridge_ref, window_ref, stamps_ref, target_ref, transfer_ref, coadd_ref,
    feats, images, target, system, right, left, inverse, sem,
):
    copies = []
    for k in range(NSEL):
        copies.append(
            pltpu.make_async_copy(window_ref.at[pair_ref[k]], feats.at[pl.ds(NPIX * k, NPIX)], sem.at[k])
        )
    fetch_target = pltpu.make_async_copy(target_ref, target, sem.at[NSEL])
    for copy in copies:
        copy.start()
    fetch_target.start()
    fetch_images = []
    for k in range(NSEL):
        fetch_images.append(pltpu.make_async_copy(stamps_ref.at[pair_ref[k]], images.at[k], sem.at[NSEL + 1 + k]))
        fetch_images[k].start()
    feats[ORDER:, :] = jnp.zeros((PADDED - ORDER, FEAT), F32)
    for copy in copies:
        copy.wait()

    system[...] = dot(feats[...], feats[...], ((1,), (1,)))
    ridge = ridge_ref[0]
    eye = jnp.where(
        lax.broadcasted_iota(jnp.int32, (TILE, TILE), 0) == lax.broadcasted_iota(jnp.int32, (TILE, TILE), 1),
        ridge, 0.0,
    )
    for k in range(NBLOCK):
        at = pl.ds(TILE * k, TILE)
        system[at, at] += eye
    fetch_target.wait()
    right[...] = dot(feats[...], target[...], ((1,), (1,)))

    def eliminate(k, carry):
        at = pl.ds(pl.multiple_of(TILE * k, TILE), TILE)
        groups = [
            system[pl.ds(pl.multiple_of(TILE * k + 8 * i, 8), 8), at] for i in range(TILE // 8)
        ]
        groups = invert_tile(groups)
        for i in range(TILE // 8):
            inverse[8 * i : 8 * i + 8, :] = groups[i]
        left[...] = dot(system[:, at], inverse[...])
        left[at, :] = -inverse[...]
        across = system[at, :]
        system[at, :] = jnp.zeros((TILE, PADDED), F32)
        left_top, left_low = halves(left[...])
        across_top, across_low = halves(across)
        change = jnp.dot(
            jnp.concatenate([left_top, left_low], axis=1),
            jnp.concatenate([across_top, across_top], axis=0),
            preferred_element_type=F32,
        )
        change += jnp.dot(left_top, across_low, preferred_element_type=F32)
        system[...] -= change
        system[:, at] = -left[...]
        return carry

    lax.fori_loop(0, NBLOCK, eliminate, 0)
    transfer = dot(system[:ORDER, :], right[...])
    transfer_ref[...] = transfer
    result = jnp.zeros((LAYERS, NOUT_PIX), F32)
    for k in range(NSEL):
        fetch_images[k].wait()
        result += dot(images[k][:, :NPIX], transfer_ref[NPIX * k : NPIX * k + NPIX, :])
    coadd_ref[...] = result


def solve(pair_list, ridge, window, stamps, target):
    return pl.pallas_call(
        solve_kernel,
        out_shape=(
            jax.ShapeDtypeStruct((ORDER, NOUT_PIX), F32),
            jax.ShapeDtypeStruct((LAYERS, NOUT_PIX), F32),
        ),
        in_specs=[
            pl.BlockSpec(memory_space=pltpu.SMEM),
            pl.BlockSpec(memory_space=pltpu.SMEM),
            pl.BlockSpec(memory_space=pl.ANY),
            pl.BlockSpec(memory_space=pl.ANY),
            pl.BlockSpec(memory_space=pl.ANY),
        ],
        out_specs=(pl.BlockSpec(memory_space=pltpu.VMEM), pl.BlockSpec(memory_space=pltpu.VMEM)),
        scratch_shapes=[
            pltpu.VMEM((PADDED, FEAT), F32),
            pltpu.VMEM((NSEL, LAYERS, TILE), F32),
            pltpu.VMEM((NOUT_PIX, FEAT), F32),
            pltpu.VMEM((PADDED, PADDED), F32),
            pltpu.VMEM((PADDED, NOUT_PIX), F32),
            pltpu.VMEM((PADDED, TILE), F32),
            pltpu.VMEM((TILE, TILE), F32),
            pltpu.SemaphoreType.DMA((2 * NSEL + 1,)),
        ],
        compiler_params=pltpu.CompilerParams(vmem_limit_bytes=48 << 20),
        name="solve_stamp",
    )(pair_list, ridge, window, stamps, target)


def blend_kernel(n_sky, n_batch, coadd_ref, out_ref, slots, send_sem, recv_sem):
    s = lax.axis_index("sky")
    b = lax.axis_index("batch")
    up = lax.rem(s + 1, n_sky)
    down = lax.rem(s + n_sky - 1, n_sky)
    right = lax.rem(b + 1, n_batch)
    left = lax.rem(b + n_batch - 1, n_batch)
    where = ((down, b), (up, b), (s, left), (s, right))
    barrier = pltpu.get_barrier_semaphore()
    for device in where:
        pl.semaphore_signal(barrier, inc=1, device_id=device, device_id_type=MESH)
    pl.semaphore_wait(barrier, 4)
    copies = [
        pltpu.make_async_remote_copy(
            src_ref=coadd_ref, dst_ref=slots.at[n], send_sem=send_sem.at[n], recv_sem=recv_sem.at[n],
            device_id=where[n], device_id_type=MESH,
        )
        for n in range(4)
    ]
    for copy in copies:
        copy.start()
    pixel = lax.broadcasted_iota(jnp.int32, (1, NOUT_PIX), 1)
    line = pixel // SIDE
    place = pixel - line * SIDE
    edge = SIDE - FADE

    def weight(at, low, first, step, there):
        value = (first + step * (at - low)).astype(F32) / (FADE + 1.0)
        value = jnp.where((at >= low) & (at < low + FADE), value, 0.0)
        return jnp.where(there, value, 0.0)

    weights = (
        weight(place, edge, 1, 1, s < n_sky - 1),
        weight(place, 0, FADE, -1, s > 0),
        weight(line, edge, 1, 1, b < n_batch - 1),
        weight(line, 0, FADE, -1, b > 0),
    )
    shifts = (edge, -edge, edge * SIDE, -edge * SIDE)
    result = coadd_ref[...]
    for n in range(4):
        copies[n].wait_recv()
        other = slots[n]
        shift = shifts[n] % NOUT_PIX
        moved = jnp.concatenate([other[:, NOUT_PIX - shift :], other[:, : NOUT_PIX - shift]], axis=1)
        result = result + weights[n] * moved
    out_ref[...] = result
    for copy in copies:
        copy.wait_send()


def blend(coadd):
    n_sky, n_batch = lax.axis_size("sky"), lax.axis_size("batch")
    return pl.pallas_call(
        functools.partial(blend_kernel, n_sky, n_batch),
        out_shape=jax.ShapeDtypeStruct((LAYERS, NOUT_PIX), F32),
        in_specs=[pl.BlockSpec(memory_space=pltpu.VMEM)],
        out_specs=pl.BlockSpec(memory_space=pltpu.VMEM),
        scratch_shapes=[
            pltpu.VMEM((4, LAYERS, NOUT_PIX), F32),
            pltpu.SemaphoreType.DMA((4,)),
            pltpu.SemaphoreType.DMA((4,)),
        ],
        compiler_params=pltpu.CompilerParams(collective_id=1, has_side_effects=True),
        name="blend_edges",
    )(coadd)


def local(features, target, images, layer_mask, pair_list, ridge_weight):
    window, stamps = gather_window(
        features.reshape(NPIX, FEAT), images.reshape(LAYERS, NPIX), layer_mask.reshape(LAYERS)
    )
    transfer, coadd = solve(
        pair_list.reshape(NSEL), ridge_weight.reshape(1), window, stamps, target.reshape(NOUT_PIX, FEAT)
    )
    final = blend(coadd)
    return (transfer.reshape(1, 1, ORDER, NOUT_PIX), final.reshape(LAYERS, SIDE, SIDE))


def solution(mesh):
    in_specs = (
        P("batch", "sky", None, None),
        P("batch", "sky", None, None),
        P("batch", "sky", None, None),
        P("batch", "sky", None),
        P("batch", "sky", None),
        P("batch", "sky"),
    )
    out_specs = (P("batch", "sky", None, None), P(None, "batch", "sky"))
    return jax.shard_map(local, mesh=mesh, in_specs=in_specs, out_specs=out_specs, check_vma=False)
```

```python
import functools

import jax
import jax.numpy as jnp
from jax import lax
from jax.experimental import pallas as pl
from jax.experimental.pallas import tpu as pltpu
from jax.sharding import PartitionSpec as P

NPIX = 80
FEAT = 1024
SIDE = 24
LAYERS = 16
NSEL = 9
FADE = 4
ORDER = 720
NOUT_PIX = 576
CAND = 12

TILE = 128
NBLOCK = 6
PADDED = TILE * NBLOCK
HALF = NPIX // 2
MESH = pl.DeviceIdType.MESH
HIGH = lax.Precision.HIGH
NT = (((1,), (1,)), ((), ()))
F32 = jnp.float32
BF16 = jnp.bfloat16


def gather_kernel(
    n_sky, n_batch, feat_ref, image_ref, mask_ref, window_ref, stamps_ref,
    masked, zeros, zero_image, local_sem, fs_sem, fr_sem, ys_sem, yr_sem, is_sem, ir_sem, js_sem, jr_sem,
):
    s = lax.axis_index("sky")
    b = lax.axis_index("batch")
    up = lax.rem(s + 1, n_sky)
    down = lax.rem(s + n_sky - 1, n_sky)
    right = lax.rem(b + 1, n_batch)
    left = lax.rem(b + n_batch - 1, n_batch)
    far = lax.rem(b + 2, n_batch)

    barrier = pltpu.get_barrier_semaphore()
    for where in ((s, left), (s, right), (up, b), (down, b)):
        pl.semaphore_signal(barrier, inc=1, device_id=where, device_id_type=MESH)

    row = lax.broadcasted_iota(jnp.int32, (LAYERS, NPIX), 0)
    keep = jnp.zeros((LAYERS, NPIX), jnp.int32)
    for layer in range(LAYERS):
        keep = jnp.where(row == layer, mask_ref[layer], keep)
    masked[...] = jnp.zeros((LAYERS, TILE), F32)
    masked[:, :NPIX] = image_ref[...] * keep.astype(F32)
    zeros[...] = jnp.zeros((NPIX, FEAT), F32)
    zero_image[...] = jnp.zeros((LAYERS, TILE), F32)

    pl.semaphore_wait(barrier, 4)

    rows = (pl.ds(0, HALF), pl.ds(HALF, HALF))

    def remote(src, dst, send, recv, where):
        return pltpu.make_async_remote_copy(
            src_ref=src, dst_ref=dst, send_sem=send, recv_sem=recv, device_id=where, device_id_type=MESH
        )

    def along(number, owner, half, where, src=None):
        slot = window_ref.at[3 * owner + 1, rows[half]]
        return remote(slot if src is None else src, slot, fs_sem.at[number], fr_sem.at[number], where)

    own_half = (feat_ref.at[rows[0]], feat_ref.at[rows[1]])
    sends = []
    for half in (0, 1):
        sends += [
            along(0 + half, b, half, (s, right), own_half[half]),
            along(2 + half, b, half, (s, left), own_half[half]),
        ]
        for copy in sends[-2:]:
            copy.start()

    def across(place, owner, half, src=None):
        base = window_ref.at[3 * owner + 1, rows[half]] if src is None else src
        number = 2 * place + half
        return (
            remote(base, window_ref.at[3 * owner, rows[half]], ys_sem.at[0, number], yr_sem.at[0, number], (up, b)),
            remote(base, window_ref.at[3 * owner + 2, rows[half]], ys_sem.at[1, number], yr_sem.at[1, number], (down, b)),
        )

    def start(copies):
        for copy in copies:
            copy.start()
        sends.extend(copies)

    for half in (0, 1):
        start(across(0, b, half, own_half[half]))

    own = [
        pltpu.make_async_copy(feat_ref, window_ref.at[3 * b + 1], local_sem.at[0]),
        pltpu.make_async_copy(masked, stamps_ref.at[3 * b + 1], local_sem.at[1]),
    ]
    for copy in own:
        copy.start()

    def image_along(number, owner, where, src):
        return remote(src, stamps_ref.at[3 * owner + 1], is_sem.at[number], ir_sem.at[number], where)

    def image_across(place, owner, src):
        return (
            remote(src, stamps_ref.at[3 * owner], js_sem.at[0, place], jr_sem.at[0, place], (up, b)),
            remote(src, stamps_ref.at[3 * owner + 2], js_sem.at[1, place], jr_sem.at[1, place], (down, b)),
        )

    start((image_along(0, b, (s, right), masked), image_along(1, b, (s, left), masked)))
    start(image_across(0, b, masked))

    along(0, left, 0, (s, left)).wait_recv()
    start((along(4, left, 0, (s, right)),))
    start(across(1, left, 0))
    along(2, right, 0, (s, right)).wait_recv()
    start(across(2, right, 0))
    along(3, right, 1, (s, right)).wait_recv()
    start((along(5, right, 1, (s, left)),))
    start(across(2, right, 1))
    along(1, left, 1, (s, left)).wait_recv()
    start(across(1, left, 1))

    image_along(0, left, (s, left), stamps_ref.at[3 * left + 1]).wait_recv()
    start((image_along(2, left, (s, right), stamps_ref.at[3 * left + 1]),))
    start(image_across(1, left, stamps_ref.at[3 * left + 1]))
    image_along(1, right, (s, right), stamps_ref.at[3 * right + 1]).wait_recv()
    start(image_across(2, right, stamps_ref.at[3 * right + 1]))
    image_along(2, far, (s, left), stamps_ref.at[3 * far + 1]).wait_recv()
    start(image_across(3, far, stamps_ref.at[3 * far + 1]))

    along(4, far, 0, (s, left)).wait_recv()
    start(across(3, far, 0))
    along(5, far, 1, (s, right)).wait_recv()
    start(across(3, far, 1))

    for place, owner in enumerate((b, left, right, far)):
        for half in (0, 1):
            for copy in across(place, owner, half):
                copy.wait_recv()
        for copy in image_across(place, owner, stamps_ref.at[3 * owner + 1]):
            copy.wait_recv()
    for copy in sends:
        copy.wait_send()
    for copy in own:
        copy.wait()

    def blank(side):
        for owner in range(n_batch):
            copy = pltpu.make_async_copy(zeros, window_ref.at[3 * owner + side], local_sem.at[0])
            other = pltpu.make_async_copy(zero_image, stamps_ref.at[3 * owner + side], local_sem.at[1])
            copy.start()
            other.start()
            copy.wait()
            other.wait()

    @pl.when(s == 0)
    def _():
        blank(0)

    @pl.when(s == n_sky - 1)
    def _():
        blank(2)


def gather_window(features, images, layer_mask):
    n_sky, n_batch = lax.axis_size("sky"), lax.axis_size("batch")
    return pl.pallas_call(
        functools.partial(gather_kernel, n_sky, n_batch),
        out_shape=(
            jax.ShapeDtypeStruct((CAND, NPIX, FEAT), F32),
            jax.ShapeDtypeStruct((CAND, LAYERS, TILE), F32),
        ),
        in_specs=[
            pl.BlockSpec(memory_space=pltpu.VMEM),
            pl.BlockSpec(memory_space=pltpu.VMEM),
            pl.BlockSpec(memory_space=pltpu.SMEM),
        ],
        out_specs=(pl.BlockSpec(memory_space=pl.ANY), pl.BlockSpec(memory_space=pl.ANY)),
        scratch_shapes=[
            pltpu.VMEM((LAYERS, TILE), F32),
            pltpu.VMEM((NPIX, FEAT), F32),
            pltpu.VMEM((LAYERS, TILE), F32),
            pltpu.SemaphoreType.DMA((2,)),
            pltpu.SemaphoreType.DMA((6,)),
            pltpu.SemaphoreType.DMA((6,)),
            pltpu.SemaphoreType.DMA((2, 8)),
            pltpu.SemaphoreType.DMA((2, 8)),
            pltpu.SemaphoreType.DMA((3,)),
            pltpu.SemaphoreType.DMA((3,)),
            pltpu.SemaphoreType.DMA((2, 4)),
            pltpu.SemaphoreType.DMA((2, 4)),
        ],
        compiler_params=pltpu.CompilerParams(collective_id=0, has_side_effects=True),
        name="gather_window",
    )(features, images, layer_mask)


def row_of(tile, index):
    return jnp.broadcast_to(tile[index : index + 1, :], (8, TILE))


def column_of(tile, index):
    return jnp.broadcast_to(tile[:, index : index + 1], (8, TILE))


def total(terms):
    while len(terms) > 1:
        terms = [terms[i] + terms[i + 1] if i + 1 < len(terms) else terms[i] for i in range(0, len(terms), 2)]
    return terms[0]


def reduce_single(block, carried, row):
    block, carried = list(block), list(carried)
    for p in range(8):
        scale = 1.0 / row_of(block[p], p)
        pivot = block[p]
        here = row == p

        def step(tile):
            scaled = row_of(tile, p) * scale
            return jnp.where(here, scaled, tile - pivot * scaled)

        for j in range(p + 1, 8):
            block[j] = step(block[j])
        carried = [step(tile) for tile in carried]
    return carried


def reduce_paired(block, carried, row):
    block, carried = list(block), list(carried)
    for p in range(0, 8, 2):
        q = p + 1
        first, mixed, second = row_of(block[p], p), row_of(block[q], p), row_of(block[q], q)
        scale = 1.0 / (first * second - mixed * mixed)
        upper, cross, lower = second * scale, mixed * scale, first * scale
        pivot_p, pivot_q = block[p], block[q]
        at_p, at_q = row == p, row == q

        def step(tile):
            x, y = row_of(tile, p), row_of(tile, q)
            new_p = upper * x - cross * y
            new_q = lower * y - cross * x
            return jnp.where(at_p, new_p, jnp.where(at_q, new_q, tile - (pivot_p * new_p + pivot_q * new_q)))

        for j in range(q + 1, 8):
            block[j] = step(block[j])
        carried = [step(tile) for tile in carried]
    return carried


def invert_tile(groups, jobs):
    row = lax.broadcasted_iota(jnp.int32, (8, TILE), 0)
    lane = lax.broadcasted_iota(jnp.int32, (8, TILE), 1)
    groups = list(groups)
    count = len(groups)
    zero = jnp.zeros((16, TILE), BF16)
    for k0 in range(0, count, 2):
        k1 = k0 + 1
        in0 = (lane >= 8 * k0) & (lane < 8 * k0 + 8)
        in1 = (lane >= 8 * k1) & (lane < 8 * k1 + 8)
        inside = in0 | in1
        top, low = groups[k0], groups[k1]
        near = [k1 + 1, k1 + 2] if k1 + 2 < count else []
        far = [i for i in range(count) if i not in near and i not in (k0, k1)]
        diag = [column_of(top, 8 * k0 + j) for j in range(8)]
        beside = [column_of(top, 8 * k1 + j) for j in range(8)]
        below = [column_of(low, 8 * k0 + j) for j in range(8)]
        corner = [column_of(low, 8 * k1 + j) for j in range(8)]
        factors = {i: [column_of(groups[i], 8 * k0 + j) for j in range(16)] for i in near}
        for job in jobs[k0 // 2 * len(jobs) * 2 // count : (k0 // 2 + 1) * len(jobs) * 2 // count]:
            job()
        panel = jnp.where(in0, jnp.where(lane - 8 * k0 == row, 1.0, 0.0), top)
        out = reduce_single(diag, beside + [panel], row)
        upper, top = out[:8], out[8]
        corner = [corner[m] - total([below[j] * row_of(upper[m], j) for j in range(8)]) for m in range(8)]
        low = jnp.where(in0, 0.0, low) - total([below[j] * row_of(top, j) for j in range(8)])
        panel = jnp.where(in1, jnp.where(lane - 8 * k1 == row, 1.0, 0.0), low)
        low = reduce_paired(corner, [panel], row)[0]
        low_rows = [row_of(low, j) for j in range(8)]
        top = jnp.where(in1, 0.0, top) - total([upper[j] * low_rows[j] for j in range(8)])
        rows = [row_of(top, j) for j in range(8)] + low_rows
        groups[k0], groups[k1] = top, low
        old = jnp.concatenate([groups[i] for i in far], axis=0)
        for i in near:
            groups[i] = jnp.where(inside, 0.0, groups[i]) - total([factors[i][j] * rows[j] for j in range(16)])
        old_top, old_low = halves(old)
        new_top, new_low = halves(jnp.concatenate([top, low], axis=0))
        before, after = [zero] * (k0 // 2), [zero] * (TILE // 16 - 1 - k0 // 2)
        new_top = jnp.concatenate(before + [new_top] + after, axis=0)
        new_low = jnp.concatenate(before + [new_low] + after, axis=0)
        change = jnp.dot(
            jnp.concatenate([old_top, old_low], axis=1),
            jnp.concatenate([new_top, new_top], axis=0),
            preferred_element_type=F32,
        ) + jnp.dot(old_top, new_low, preferred_element_type=F32)
        for n, i in enumerate(far):
            groups[i] = jnp.where(inside, 0.0, groups[i]) - change[8 * n : 8 * n + 8]
    return groups


def dot(a, b, dims=((1,), (0,))):
    return lax.dot_general(a, b, (dims, ((), ())), precision=HIGH, preferred_element_type=F32)


def halves(x):
    top = x.astype(BF16)
    return top, (x - top.astype(F32)).astype(BF16)


def solve_kernel(
    pair_ref, ridge_ref, window_ref, stamps_ref, target_ref, transfer_ref, coadd_ref,
    feats, images, target, feat_top, feat_low, target_top, target_low, system, right,
    left_top, left_low, across_top, across_low, diag, inverse, previous, sem,
):
    copies = []
    for k in range(NSEL):
        copies.append(
            pltpu.make_async_copy(window_ref.at[pair_ref[k]], feats.at[pl.ds(NPIX * k, NPIX)], sem.at[k])
        )
    fetch_target = pltpu.make_async_copy(target_ref, target, sem.at[NSEL])
    for copy in copies:
        copy.start()
    fetch_images = []
    for k in range(NSEL):
        fetch_images.append(pltpu.make_async_copy(stamps_ref.at[pair_ref[k]], images.at[k], sem.at[NSEL + 1 + k]))
        fetch_images[k].start()
    fetch_target.start()
    feat_top[ORDER:, :] = jnp.zeros((PADDED - ORDER, FEAT), BF16)
    feat_low[ORDER:, :] = jnp.zeros((PADDED - ORDER, FEAT), BF16)
    for k in range(NSEL):
        copies[k].wait()
        rows = pl.ds(NPIX * k, NPIX)
        feat_top[rows, :], feat_low[rows, :] = halves(feats[rows, :])

    def product(a_top, a_low, b_top, b_low):
        result = lax.dot_general(a_top, b_top, NT, preferred_element_type=F32)
        result += lax.dot_general(a_top, b_low, NT, preferred_element_type=F32)
        return result + lax.dot_general(a_low, b_top, NT, preferred_element_type=F32)

    wide = 2 * TILE
    for k in range(PADDED // wide):
        rows, rest = pl.ds(wide * k, wide), pl.ds(wide * k, PADDED - wide * k)
        system[rows, rest] = product(feat_top[rows, :], feat_low[rows, :], feat_top[rest, :], feat_low[rest, :])
    for k in range(PADDED // wide):
        for j in range(k):
            rows, columns = pl.ds(wide * k, wide), pl.ds(wide * j, wide)
            system[rows, columns] = system[columns, rows].T
    ridge = ridge_ref[0]
    eye = jnp.where(
        lax.broadcasted_iota(jnp.int32, (TILE, TILE), 0) == lax.broadcasted_iota(jnp.int32, (TILE, TILE), 1),
        ridge, 0.0,
    )
    for k in range(NBLOCK):
        at = pl.ds(TILE * k, TILE)
        system[at, at] += eye
    diag[...] = system[:TILE, :TILE]
    fetch_target.wait()
    for copy in fetch_images:
        copy.wait()

    third = PADDED // 3

    def left_job(j, part):
        def job():
            at = pl.ds(pl.multiple_of(TILE * j, TILE), TILE)
            rows = pl.ds(third * part, third)
            left = dot(system[rows, at], previous[...])
            system[rows, at] = -left
            left_top[rows, :], left_low[rows, :] = halves(left)
        return job

    def across_job(j):
        def job():
            at = pl.ds(pl.multiple_of(TILE * j, TILE), TILE)
            across_top[...], across_low[...] = halves(system[at, :])
            system[at, :] = jnp.zeros((TILE, PADDED), F32)
            system[at, at] = previous[...]
            top, low = halves(-previous[...])
            left_top[at, :] = top
            left_low[at, :] = low
            across_top[:, at] = jnp.zeros((TILE, TILE), BF16)
            across_low[:, at] = jnp.zeros((TILE, TILE), BF16)
        return job

    def update_job(part):
        def job():
            columns = pl.ds(third * part, third)
            top = across_top[:, columns]
            change = jnp.dot(
                jnp.concatenate([left_top[...], left_low[...]], axis=1),
                jnp.concatenate([top, top], axis=0),
                preferred_element_type=F32,
            )
            change += jnp.dot(left_top[...], across_low[:, columns], preferred_element_type=F32)
            system[:, columns] -= change
        return job

    def split_job(part):
        def job():
            rows = pl.ds(NOUT_PIX // 3 * part, NOUT_PIX // 3)
            target_top[rows, :], target_low[rows, :] = halves(target[rows, :])
        return job

    def right_job(j, part):
        def job():
            at = pl.ds(pl.multiple_of(TILE * j, TILE), TILE)
            share = NOUT_PIX // 3
            rows = pl.ds(share * part, share)
            right[rows, at] = product(target_top[rows, :], target_low[rows, :], feat_top[at, :], feat_low[at, :])
        return job

    def invert(rows, jobs):
        groups = invert_tile([diag[8 * i : 8 * i + 8, :] for i in range(rows // 8)], jobs)
        for i, group in enumerate(groups):
            inverse[8 * i : 8 * i + 8, :] = group

    def advance(k):
        at = pl.ds(pl.multiple_of(TILE * k, TILE), TILE)
        then = pl.ds(pl.multiple_of(TILE * k + TILE, TILE), TILE)
        diag[...] = system[then, then] - dot(dot(system[then, at], inverse[...]), system[at, then])
        previous[...] = inverse[...]

    def jobs_after(j):
        return [left_job(j, part) for part in range(3)] + [across_job(j)] + [update_job(part) for part in range(3)]

    invert(TILE, [split_job(part) for part in range(3)] + [right_job(0, part) for part in range(3)])
    advance(0)

    def eliminate(k, carry):
        invert(TILE, jobs_after(k - 1) + [right_job(k, part) for part in range(3)])
        advance(k)
        return carry

    lax.fori_loop(1, NBLOCK - 1, eliminate, 0)
    last = NBLOCK - 1
    inverse[...] = jnp.zeros((TILE, TILE), F32)
    invert(ORDER - TILE * last, jobs_after(last - 1) + [right_job(last, part) for part in range(3)])
    previous[...] = inverse[...]
    for job in jobs_after(last):
        job()
    transfer = dot(right[...], system[...])
    transfer_ref[...] = transfer[:, :ORDER]

    empty = jnp.zeros((LAYERS, TILE), F32)
    strips = [empty] * (NBLOCK + 1)
    for k in range(NSEL):
        first, shift = divmod(NPIX * k, TILE)
        wide = jnp.concatenate([images[k], empty], axis=1)
        if shift:
            wide = pltpu.roll(wide, shift, 1)
        strips[first] = strips[first] + wide[:, :TILE]
        strips[first + 1] = strips[first + 1] + wide[:, TILE:]
    coadd_ref[...] = dot(jnp.concatenate(strips[:NBLOCK], axis=1), transfer, ((1,), (1,)))


def solve(pair_list, ridge, window, stamps, target):
    return pl.pallas_call(
        solve_kernel,
        out_shape=(
            jax.ShapeDtypeStruct((NOUT_PIX, ORDER), F32),
            jax.ShapeDtypeStruct((LAYERS, NOUT_PIX), F32),
        ),
        in_specs=[
            pl.BlockSpec(memory_space=pltpu.SMEM),
            pl.BlockSpec(memory_space=pltpu.SMEM),
            pl.BlockSpec(memory_space=pltpu.HBM),
            pl.BlockSpec(memory_space=pltpu.HBM),
            pl.BlockSpec(memory_space=pltpu.HBM),
        ],
        out_specs=(pl.BlockSpec(memory_space=pltpu.VMEM), pl.BlockSpec(memory_space=pltpu.VMEM)),
        scratch_shapes=[
            pltpu.VMEM((PADDED, FEAT), F32),
            pltpu.VMEM((NSEL, LAYERS, TILE), F32),
            pltpu.VMEM((NOUT_PIX, FEAT), F32),
            pltpu.VMEM((PADDED, FEAT), BF16),
            pltpu.VMEM((PADDED, FEAT), BF16),
            pltpu.VMEM((NOUT_PIX, FEAT), BF16),
            pltpu.VMEM((NOUT_PIX, FEAT), BF16),
            pltpu.VMEM((PADDED, PADDED), F32),
            pltpu.VMEM((NOUT_PIX, PADDED), F32),
            pltpu.VMEM((PADDED, TILE), BF16),
            pltpu.VMEM((PADDED, TILE), BF16),
            pltpu.VMEM((TILE, PADDED), BF16),
            pltpu.VMEM((TILE, PADDED), BF16),
            pltpu.VMEM((TILE, TILE), F32),
            pltpu.VMEM((TILE, TILE), F32),
            pltpu.VMEM((TILE, TILE), F32),
            pltpu.SemaphoreType.DMA((2 * NSEL + 1,)),
        ],
        compiler_params=pltpu.CompilerParams(vmem_limit_bytes=56 << 20),
        name="solve_stamp",
    )(pair_list, ridge, window, stamps, target)


def blend_kernel(n_sky, n_batch, coadd_ref, out_ref, slots, send_sem, recv_sem):
    s = lax.axis_index("sky")
    b = lax.axis_index("batch")
    up = lax.rem(s + 1, n_sky)
    down = lax.rem(s + n_sky - 1, n_sky)
    right = lax.rem(b + 1, n_batch)
    left = lax.rem(b + n_batch - 1, n_batch)
    where = ((down, b), (up, b), (s, left), (s, right))
    barrier = pltpu.get_barrier_semaphore()
    for device in where:
        pl.semaphore_signal(barrier, inc=1, device_id=device, device_id_type=MESH)
    pl.semaphore_wait(barrier, 4)
    copies = [
        pltpu.make_async_remote_copy(
            src_ref=coadd_ref, dst_ref=slots.at[n], send_sem=send_sem.at[n], recv_sem=recv_sem.at[n],
            device_id=where[n], device_id_type=MESH,
        )
        for n in range(4)
    ]
    for copy in copies:
        copy.start()
    pixel = lax.broadcasted_iota(jnp.int32, (1, NOUT_PIX), 1)
    line = pixel // SIDE
    place = pixel - line * SIDE
    edge = SIDE - FADE

    def weight(at, low, first, step, there):
        value = (first + step * (at - low)).astype(F32) / (FADE + 1.0)
        value = jnp.where((at >= low) & (at < low + FADE), value, 0.0)
        return jnp.where(there, value, 0.0)

    weights = (
        weight(place, edge, 1, 1, s < n_sky - 1),
        weight(place, 0, FADE, -1, s > 0),
        weight(line, edge, 1, 1, b < n_batch - 1),
        weight(line, 0, FADE, -1, b > 0),
    )
    shifts = (edge, -edge, edge * SIDE, -edge * SIDE)
    result = coadd_ref[...]
    for n in range(4):
        copies[n].wait_recv()
        other = slots[n]
        shift = shifts[n] % NOUT_PIX
        moved = jnp.concatenate([other[:, NOUT_PIX - shift :], other[:, : NOUT_PIX - shift]], axis=1)
        result = result + weights[n] * moved
    out_ref[...] = result
    for copy in copies:
        copy.wait_send()


def blend(coadd):
    n_sky, n_batch = lax.axis_size("sky"), lax.axis_size("batch")
    return pl.pallas_call(
        functools.partial(blend_kernel, n_sky, n_batch),
        out_shape=jax.ShapeDtypeStruct((LAYERS, NOUT_PIX), F32),
        in_specs=[pl.BlockSpec(memory_space=pltpu.VMEM)],
        out_specs=pl.BlockSpec(memory_space=pltpu.VMEM),
        scratch_shapes=[
            pltpu.VMEM((4, LAYERS, NOUT_PIX), F32),
            pltpu.SemaphoreType.DMA((4,)),
            pltpu.SemaphoreType.DMA((4,)),
        ],
        compiler_params=pltpu.CompilerParams(collective_id=1, has_side_effects=True),
        name="blend_edges",
    )(coadd)


def local(features, target, images, layer_mask, pair_list, ridge_weight):
    window, stamps = gather_window(
        features.reshape(NPIX, FEAT), images.reshape(LAYERS, NPIX), layer_mask.reshape(LAYERS)
    )
    transfer, coadd = solve(
        pair_list.reshape(NSEL), ridge_weight.reshape(1), window, stamps, target.reshape(NOUT_PIX, FEAT)
    )
    final = blend(coadd)
    return (transfer.T.reshape(1, 1, ORDER, NOUT_PIX), final.reshape(LAYERS, SIDE, SIDE))


def solution(mesh):
    in_specs = (
        P("batch", "sky", None, None),
        P("batch", "sky", None, None),
        P("batch", "sky", None, None),
        P("batch", "sky", None),
        P("batch", "sky", None),
        P("batch", "sky"),
    )
    out_specs = (P("batch", "sky", None, None), P(None, "batch", "sky"))
    return jax.shard_map(local, mesh=mesh, in_specs=in_specs, out_specs=out_specs, check_vma=False)
```

```python
import functools

import jax
import jax.numpy as jnp
from jax import lax
from jax.experimental import pallas as pl
from jax.experimental.pallas import tpu as pltpu
from jax.sharding import PartitionSpec as P

NPIX = 80
FEAT = 1024
SIDE = 24
LAYERS = 16
NSEL = 9
FADE = 4
ORDER = 720
NOUT_PIX = 576
CAND = 12

TILE = 128
NBLOCK = 6
PADDED = TILE * NBLOCK
PARTS = (pl.ds(0, 24), pl.ds(24, 16), pl.ds(40, 24), pl.ds(64, 16))
MESH = pl.DeviceIdType.MESH
HIGH = lax.Precision.HIGH
NT = (((1,), (1,)), ((), ()))
F32 = jnp.float32
BF16 = jnp.bfloat16


def halves(x):
    top = x.astype(BF16)
    return top, (x - top.astype(F32)).astype(BF16)


def gather_kernel(
    n_sky, n_batch, feat_ref, image_ref, mask_ref, target_ref, top_ref, low_ref, stamps_ref, target_top_ref, target_low_ref,
    window, target, masked, top, low, target_top, target_low, local_sem, out_sem, fs_sem, fr_sem, ys_sem, yr_sem, is_sem, ir_sem, js_sem, jr_sem,
):
    s = lax.axis_index("sky")
    b = lax.axis_index("batch")
    up = lax.rem(s + 1, n_sky)
    down = lax.rem(s + n_sky - 1, n_sky)
    right = lax.rem(b + 1, n_batch)
    left = lax.rem(b + n_batch - 1, n_batch)
    far = lax.rem(b + 2, n_batch)

    barrier = pltpu.get_barrier_semaphore()
    for where in ((s, left), (s, right), (up, b), (down, b)):
        pl.semaphore_signal(barrier, inc=1, device_id=where, device_id_type=MESH)
    fetch_target = pltpu.make_async_copy(target_ref, target, local_sem.at[0])
    fetch_target.start()
    fetch_own = pltpu.make_async_copy(feat_ref, window.at[3 * b + 1], local_sem.at[1])
    fetch_own.start()

    row = lax.broadcasted_iota(jnp.int32, (LAYERS, NPIX), 0)
    keep = jnp.zeros((LAYERS, NPIX), jnp.int32)
    for layer in range(LAYERS):
        keep = jnp.where(row == layer, mask_ref[layer], keep)
    masked[...] = jnp.zeros((LAYERS, TILE), F32)
    masked[:, :NPIX] = image_ref[...] * keep.astype(F32)

    pl.semaphore_wait(barrier, 4)

    def remote(src, dst, send, recv, where):
        return pltpu.make_async_remote_copy(
            src_ref=src, dst_ref=dst, send_sem=send, recv_sem=recv, device_id=where, device_id_type=MESH
        )

    def along(direction, number, owner, part, src=None):
        slot = window.at[3 * owner + 1, PARTS[part]]
        where = (s, left) if direction else (s, right)
        return remote(
            slot if src is None else src, slot, fs_sem.at[direction, number], fr_sem.at[direction, number], where
        )

    def across(place, owner, part, src=None):
        base = window.at[3 * owner + 1, PARTS[part]] if src is None else src
        number = 4 * place + part
        return (
            remote(base, window.at[3 * owner, PARTS[part]], ys_sem.at[0, number], yr_sem.at[0, number], (up, b)),
            remote(base, window.at[3 * owner + 2, PARTS[part]], ys_sem.at[1, number], yr_sem.at[1, number], (down, b)),
        )

    def image_along(number, owner, where, src):
        return remote(src, stamps_ref.at[3 * owner + 1], is_sem.at[number], ir_sem.at[number], where)

    def image_across(place, owner, src):
        return (
            remote(src, stamps_ref.at[3 * owner], js_sem.at[0, place], jr_sem.at[0, place], (up, b)),
            remote(src, stamps_ref.at[3 * owner + 2], js_sem.at[1, place], jr_sem.at[1, place], (down, b)),
        )

    sends = []

    def start(*copies):
        for copy in copies:
            copy.start()
        sends.extend(copies)

    start(image_along(0, b, (s, right), masked), image_along(1, b, (s, left), masked))
    for part in range(4):
        own = feat_ref.at[PARTS[part]]
        start(along(0, part, b, part, own), along(1, part, b, 3 - part, feat_ref.at[PARTS[3 - part]]))
        start(*across(0, b, part, own))
    start(*image_across(0, b, masked))
    stamps_ref[3 * b + 1] = masked[...]

    def convert(slot, part, values, blank=None):
        if blank is not None:
            values = jnp.where(blank, 0.0, values)
        rows = PARTS[part]
        top[slot, rows, :], low[slot, rows, :] = halves(values)

    leaving = []

    def leave(source, out, sem):
        copy = pltpu.make_async_copy(source, out, sem)
        copy.start()
        leaving.append(copy)

    def ship(slot, number):
        leave(top.at[slot], top_ref.at[slot], out_sem.at[0, number])
        leave(low.at[slot], low_ref.at[slot], out_sem.at[1, number])

    def settle(place, owner):
        for part in range(4):
            for copy in across(place, owner, part):
                copy.wait_recv()
            convert(3 * owner, part, window[3 * owner, PARTS[part], :], s == 0)
            convert(3 * owner + 2, part, window[3 * owner + 2, PARTS[part], :], s == n_sky - 1)
        ship(3 * owner, 3 * place)
        ship(3 * owner + 2, 3 * place + 2)
        for copy in image_across(place, owner, masked):
            copy.wait_recv()
        stamps_ref[3 * owner] = jnp.where(s == 0, 0.0, stamps_ref[3 * owner])
        stamps_ref[3 * owner + 2] = jnp.where(s == n_sky - 1, 0.0, stamps_ref[3 * owner + 2])

    for part in (0, 1):
        along(0, part, left, part).wait_recv()
        start(along(0, 4 + part, left, part))
        start(*across(1, left, part))
        along(1, part, right, 3 - part).wait_recv()
        start(along(1, 4 + part, right, 3 - part))
        start(*across(2, right, 3 - part))
    image_along(0, left, (s, left), masked).wait_recv()
    start(image_along(2, left, (s, right), stamps_ref.at[3 * left + 1]))
    start(*image_across(1, left, stamps_ref.at[3 * left + 1]))
    image_along(1, right, (s, right), masked).wait_recv()
    start(*image_across(2, right, stamps_ref.at[3 * right + 1]))
    fetch_own.wait()
    for part in range(4):
        convert(3 * b + 1, part, window[3 * b + 1, PARTS[part], :])
    ship(3 * b + 1, 1)
    for part in (2, 3):
        along(0, part, left, part).wait_recv()
        start(*across(1, left, part))
        along(1, part, right, 3 - part).wait_recv()
        start(*across(2, right, 3 - part))
    image_along(2, far, (s, left), masked).wait_recv()
    start(*image_across(3, far, stamps_ref.at[3 * far + 1]))
    fetch_target.wait()
    target_top[...], target_low[...] = halves(target[...])
    leave(target_top, target_top_ref, out_sem.at[0, CAND])
    leave(target_low, target_low_ref, out_sem.at[1, CAND])
    for part in (0, 1):
        along(0, 4 + part, far, part).wait_recv()
        start(*across(3, far, part))
        along(1, 4 + part, far, 3 - part).wait_recv()
        start(*across(3, far, 3 - part))
    for place, owner in enumerate((left, right, far)):
        for part in range(4):
            convert(3 * owner + 1, part, window[3 * owner + 1, PARTS[part], :])
        ship(3 * owner + 1, 3 * place + 4)
    for place, owner in enumerate((b, left, right, far)):
        settle(place, owner)
    for copy in sends:
        copy.wait_send()
    for copy in leaving:
        copy.wait()


def gather_window(features, images, layer_mask, target):
    n_sky, n_batch = lax.axis_size("sky"), lax.axis_size("batch")
    vmem, hbm = pl.BlockSpec(memory_space=pltpu.VMEM), pl.BlockSpec(memory_space=pltpu.HBM)
    return pl.pallas_call(
        functools.partial(gather_kernel, n_sky, n_batch),
        out_shape=(
            jax.ShapeDtypeStruct((CAND, NPIX, FEAT), BF16),
            jax.ShapeDtypeStruct((CAND, NPIX, FEAT), BF16),
            jax.ShapeDtypeStruct((CAND, LAYERS, TILE), F32),
            jax.ShapeDtypeStruct((NOUT_PIX, FEAT), BF16),
            jax.ShapeDtypeStruct((NOUT_PIX, FEAT), BF16),
        ),
        in_specs=[
            pl.BlockSpec(memory_space=pltpu.HBM),
            vmem,
            pl.BlockSpec(memory_space=pltpu.SMEM),
            pl.BlockSpec(memory_space=pltpu.HBM),
        ],
        out_specs=(hbm, hbm, vmem, hbm, hbm),
        scratch_shapes=[
            pltpu.VMEM((CAND, NPIX, FEAT), F32),
            pltpu.VMEM((NOUT_PIX, FEAT), F32),
            pltpu.VMEM((LAYERS, TILE), F32),
            pltpu.VMEM((CAND, NPIX, FEAT), BF16),
            pltpu.VMEM((CAND, NPIX, FEAT), BF16),
            pltpu.VMEM((NOUT_PIX, FEAT), BF16),
            pltpu.VMEM((NOUT_PIX, FEAT), BF16),
            pltpu.SemaphoreType.DMA((2,)),
            pltpu.SemaphoreType.DMA((2, CAND + 1)),
            pltpu.SemaphoreType.DMA((2, 6)),
            pltpu.SemaphoreType.DMA((2, 6)),
            pltpu.SemaphoreType.DMA((2, 16)),
            pltpu.SemaphoreType.DMA((2, 16)),
            pltpu.SemaphoreType.DMA((3,)),
            pltpu.SemaphoreType.DMA((3,)),
            pltpu.SemaphoreType.DMA((2, 4)),
            pltpu.SemaphoreType.DMA((2, 4)),
        ],
        compiler_params=pltpu.CompilerParams(
            collective_id=0, has_side_effects=True, vmem_limit_bytes=60 << 20
        ),
        name="gather_window",
    )(features, images, layer_mask, target)


def row_of(tile, index):
    return jnp.broadcast_to(tile[index : index + 1, :], (8, TILE))


def column_of(tile, index):
    return jnp.broadcast_to(tile[:, index : index + 1], (8, TILE))


def total(terms):
    while len(terms) > 1:
        terms = [terms[i] + terms[i + 1] if i + 1 < len(terms) else terms[i] for i in range(0, len(terms), 2)]
    return terms[0]


def reduce_single(block, carried, row):
    block, carried = list(block), list(carried)
    for p in range(8):
        scale = 1.0 / row_of(block[p], p)
        pivot = block[p]
        here = row == p

        def step(tile):
            scaled = row_of(tile, p) * scale
            return jnp.where(here, scaled, tile - pivot * scaled)

        for j in range(p + 1, 8):
            block[j] = step(block[j])
        carried = [step(tile) for tile in carried]
    return carried


def reduce_paired(block, carried, row):
    block, carried = list(block), list(carried)
    for p in range(0, 8, 2):
        q = p + 1
        first, mixed, second = row_of(block[p], p), row_of(block[q], p), row_of(block[q], q)
        scale = 1.0 / (first * second - mixed * mixed)
        upper, cross, lower = second * scale, mixed * scale, first * scale
        pivot_p, pivot_q = block[p], block[q]
        at_p, at_q = row == p, row == q

        def step(tile):
            x, y = row_of(tile, p), row_of(tile, q)
            new_p = upper * x - cross * y
            new_q = lower * y - cross * x
            return jnp.where(at_p, new_p, jnp.where(at_q, new_q, tile - (pivot_p * new_p + pivot_q * new_q)))

        for j in range(q + 1, 8):
            block[j] = step(block[j])
        carried = [step(tile) for tile in carried]
    return carried


def invert_tile(groups, jobs):
    row = lax.broadcasted_iota(jnp.int32, (8, TILE), 0)
    lane = lax.broadcasted_iota(jnp.int32, (8, TILE), 1)
    groups = list(groups)
    count = len(groups)
    zero = jnp.zeros((16, TILE), BF16)
    for k0 in range(0, count, 2):
        k1 = k0 + 1
        in0 = (lane >= 8 * k0) & (lane < 8 * k0 + 8)
        in1 = (lane >= 8 * k1) & (lane < 8 * k1 + 8)
        inside = in0 | in1
        top, low = groups[k0], groups[k1]
        near = [k1 + 1, k1 + 2] if k1 + 2 < count else []
        far = [i for i in range(count) if i not in near and i not in (k0, k1)]
        diag = [column_of(top, 8 * k0 + j) for j in range(8)]
        beside = [column_of(top, 8 * k1 + j) for j in range(8)]
        below = [column_of(low, 8 * k0 + j) for j in range(8)]
        corner = [column_of(low, 8 * k1 + j) for j in range(8)]
        factors = {i: [column_of(groups[i], 8 * k0 + j) for j in range(16)] for i in near}
        for job in jobs[k0 // 2 * len(jobs) * 2 // count : (k0 // 2 + 1) * len(jobs) * 2 // count]:
            job()
        panel = jnp.where(in0, jnp.where(lane - 8 * k0 == row, 1.0, 0.0), top)
        out = reduce_single(diag, beside + [panel], row)
        upper, top = out[:8], out[8]
        corner = [corner[m] - total([below[j] * row_of(upper[m], j) for j in range(8)]) for m in range(8)]
        low = jnp.where(in0, 0.0, low) - total([below[j] * row_of(top, j) for j in range(8)])
        panel = jnp.where(in1, jnp.where(lane - 8 * k1 == row, 1.0, 0.0), low)
        low = reduce_paired(corner, [panel], row)[0]
        low_rows = [row_of(low, j) for j in range(8)]
        top = jnp.where(in1, 0.0, top) - total([upper[j] * low_rows[j] for j in range(8)])
        rows = [row_of(top, j) for j in range(8)] + low_rows
        groups[k0], groups[k1] = top, low
        old = jnp.concatenate([groups[i] for i in far], axis=0)
        for i in near:
            groups[i] = jnp.where(inside, 0.0, groups[i]) - total([factors[i][j] * rows[j] for j in range(16)])
        old_top, old_low = halves(old)
        new_top, new_low = halves(jnp.concatenate([top, low], axis=0))
        before, after = [zero] * (k0 // 2), [zero] * (TILE // 16 - 1 - k0 // 2)
        new_top = jnp.concatenate(before + [new_top] + after, axis=0)
        new_low = jnp.concatenate(before + [new_low] + after, axis=0)
        change = jnp.dot(
            jnp.concatenate([old_top, old_low], axis=1),
            jnp.concatenate([new_top, new_top], axis=0),
            preferred_element_type=F32,
        ) + jnp.dot(old_top, new_low, preferred_element_type=F32)
        for n, i in enumerate(far):
            groups[i] = jnp.where(inside, 0.0, groups[i]) - change[8 * n : 8 * n + 8]
    return groups


def dot(a, b, dims=((1,), (0,))):
    return lax.dot_general(a, b, (dims, ((), ())), precision=HIGH, preferred_element_type=F32)


def solve_kernel(
    pair_ref, ridge_ref, top_ref, low_ref, stamps_ref, target_top_ref, target_low_ref, transfer_ref, coadd_ref,
    feat_top, feat_low, target_top, target_low, system, right,
    left_top, left_low, across_top, across_low, column_top, column_low, right_top, right_low, diag, inverse, previous, result, sem,
):
    copies = []
    for k in range(NSEL):
        rows = pl.ds(NPIX * k, NPIX)
        copies.append(pltpu.make_async_copy(top_ref.at[pair_ref[k]], feat_top.at[rows], sem.at[k]))
        copies.append(pltpu.make_async_copy(low_ref.at[pair_ref[k]], feat_low.at[rows], sem.at[NSEL + k]))
    later = [
        pltpu.make_async_copy(target_top_ref, target_top, sem.at[2 * NSEL]),
        pltpu.make_async_copy(target_low_ref, target_low, sem.at[2 * NSEL + 1]),
    ]
    for copy in copies + later:
        copy.start()
    feat_top[ORDER:, :] = jnp.zeros((PADDED - ORDER, FEAT), BF16)
    feat_low[ORDER:, :] = jnp.zeros((PADDED - ORDER, FEAT), BF16)
    for copy in copies:
        copy.wait()

    def product(a_top, a_low, b_top, b_low):
        result = lax.dot_general(a_top, b_top, NT, preferred_element_type=F32)
        result += lax.dot_general(a_top, b_low, NT, preferred_element_type=F32)
        return result + lax.dot_general(a_low, b_top, NT, preferred_element_type=F32)

    wide = 2 * TILE
    for k in range(PADDED // wide):
        rows, rest = pl.ds(wide * k, wide), pl.ds(wide * k, PADDED - wide * k)
        system[rows, rest] = product(feat_top[rows, :], feat_low[rows, :], feat_top[rest, :], feat_low[rest, :])
    for k in range(PADDED // wide):
        for j in range(k):
            rows, columns = pl.ds(wide * k, wide), pl.ds(wide * j, wide)
            system[rows, columns] = system[columns, rows].T
    ridge = ridge_ref[0]
    eye = jnp.where(
        lax.broadcasted_iota(jnp.int32, (TILE, TILE), 0) == lax.broadcasted_iota(jnp.int32, (TILE, TILE), 1),
        ridge, 0.0,
    )
    for k in range(NBLOCK):
        at = pl.ds(TILE * k, TILE)
        system[at, at] += eye
    diag[...] = system[:TILE, :TILE]

    for copy in later:
        copy.wait()
    third = PADDED // 3
    share = NOUT_PIX // 3

    def block(k):
        return pl.ds(TILE * k, TILE)

    def product_of_halves(a_top, a_low, b_top, b_low):
        result = lax.dot_general(
            jnp.concatenate([a_top, a_low], axis=1), jnp.concatenate([b_top, b_top], axis=1), NT,
            preferred_element_type=F32,
        )
        return result + lax.dot_general(a_top, b_low, NT, preferred_element_type=F32)

    def right_job(part, half):
        def job():
            rows, at = pl.ds(share * part, share), pl.ds(PADDED // 2 * half, PADDED // 2)
            right[rows, at] = product(target_top[rows, :], target_low[rows, :], feat_top[at, :], feat_low[at, :])
        return job

    def take_job(j):
        def job():
            at = block(j)
            across_top[...], across_low[...] = halves(system[at, :])
            system[at, :] = jnp.zeros((TILE, PADDED), F32)
            column_top[...], column_low[...] = halves(system[:, at])
        return job

    def left_job(j, part):
        def job():
            rows = pl.ds(third * part, third)
            left = dot(system[rows, block(j)], previous[...])
            left_top[rows, :], left_low[rows, :] = halves(left)
            if third * part <= TILE * j < third * part + third:
                left_top[block(j), :], left_low[block(j), :] = halves(-previous[...])
        return job

    def update_job(j, part):
        def job():
            first = max(third * part, TILE * (j + 1))
            columns = pl.ds(first, third * part + third - first)
            top = across_top[:, columns]
            change = jnp.dot(
                jnp.concatenate([left_top[...], left_low[...]], axis=1),
                jnp.concatenate([top, top], axis=0),
                preferred_element_type=F32,
            )
            change += jnp.dot(left_top[...], across_low[:, columns], preferred_element_type=F32)
            system[:, columns] -= change
        return job

    def scale_job(j):
        def job():
            scaled = dot(right[:, block(j)], previous[...])
            right[:, block(j)] = scaled
            right_top[...], right_low[...] = halves(scaled)
        return job

    def right_update_job(j, part):
        def job():
            columns = pl.ds(third * part, third)
            right[:, columns] -= product_of_halves(
                right_top[...], right_low[...], column_top[columns, :], column_low[columns, :]
            )
        return job

    def invert(rows, jobs):
        groups = invert_tile([diag[8 * i : 8 * i + 8, :] for i in range(rows // 8)], jobs)
        for i, group in enumerate(groups):
            inverse[8 * i : 8 * i + 8, :] = group

    def advance(k):
        at, then = block(k), block(k + 1)
        diag[...] = system[then, then] - dot(dot(system[then, at], inverse[...]), system[at, then])
        previous[...] = inverse[...]

    def jobs_after(j):
        jobs = [take_job(j)] + [left_job(j, part) for part in range(3)]
        jobs += [update_job(j, part) for part in range(3) if third * part + third > TILE * (j + 1)]
        return jobs + [scale_job(j)] + [right_update_job(j, part) for part in range(3)]

    invert(TILE, [right_job(part, half) for part in range(3) for half in (0, 1)])
    advance(0)
    for k in range(1, NBLOCK - 1):
        invert(TILE, jobs_after(k - 1))
        advance(k)
    last = NBLOCK - 1
    inverse[...] = jnp.zeros((TILE, TILE), F32)
    invert(ORDER - TILE * last, jobs_after(last - 1))
    column_top[...], column_low[...] = halves(system[:, block(last)])
    outgoing = []
    for part in range(3):
        rows = pl.ds(share * part, share)
        scaled = dot(right[rows, block(last)], inverse[...])
        top, low = halves(scaled)
        head = pl.ds(0, TILE * last)
        right[rows, head] -= product_of_halves(top, low, column_top[head, :], column_low[head, :])
        right[rows, block(last)] = scaled
        result[rows, :] = right[rows, pl.ds(0, ORDER)]
        copy = pltpu.make_async_copy(result.at[rows], transfer_ref.at[rows], sem.at[part])
        copy.start()
        outgoing.append(copy)

    empty = jnp.zeros((LAYERS, TILE), F32)
    strips = [empty] * (NBLOCK + 1)
    for k in range(NSEL):
        first, shift = divmod(NPIX * k, TILE)
        wide = jnp.concatenate([stamps_ref[pair_ref[k]], empty], axis=1)
        if shift:
            wide = pltpu.roll(wide, shift, 1)
        strips[first] = strips[first] + wide[:, :TILE]
        strips[first + 1] = strips[first + 1] + wide[:, TILE:]
    coadd_ref[...] = dot(jnp.concatenate(strips[:NBLOCK], axis=1), right[...], ((1,), (1,)))
    for copy in outgoing:
        copy.wait()


def solve(pair_list, ridge, *arrays):
    return pl.pallas_call(
        solve_kernel,
        out_shape=(
            jax.ShapeDtypeStruct((NOUT_PIX, ORDER), F32),
            jax.ShapeDtypeStruct((LAYERS, NOUT_PIX), F32),
        ),
        in_specs=[
            pl.BlockSpec(memory_space=pltpu.SMEM),
            pl.BlockSpec(memory_space=pltpu.SMEM),
            pl.BlockSpec(memory_space=pltpu.HBM),
            pl.BlockSpec(memory_space=pltpu.HBM),
            pl.BlockSpec(memory_space=pltpu.VMEM),
            pl.BlockSpec(memory_space=pltpu.HBM),
            pl.BlockSpec(memory_space=pltpu.HBM),
        ],
        out_specs=(pl.BlockSpec(memory_space=pltpu.HBM), pl.BlockSpec(memory_space=pltpu.VMEM)),
        scratch_shapes=[
            pltpu.VMEM((PADDED, FEAT), BF16),
            pltpu.VMEM((PADDED, FEAT), BF16),
            pltpu.VMEM((NOUT_PIX, FEAT), BF16),
            pltpu.VMEM((NOUT_PIX, FEAT), BF16),
            pltpu.VMEM((PADDED, PADDED), F32),
            pltpu.VMEM((NOUT_PIX, PADDED), F32),
            pltpu.VMEM((PADDED, TILE), BF16),
            pltpu.VMEM((PADDED, TILE), BF16),
            pltpu.VMEM((TILE, PADDED), BF16),
            pltpu.VMEM((TILE, PADDED), BF16),
            pltpu.VMEM((PADDED, TILE), BF16),
            pltpu.VMEM((PADDED, TILE), BF16),
            pltpu.VMEM((NOUT_PIX, TILE), BF16),
            pltpu.VMEM((NOUT_PIX, TILE), BF16),
            pltpu.VMEM((TILE, TILE), F32),
            pltpu.VMEM((TILE, TILE), F32),
            pltpu.VMEM((TILE, TILE), F32),
            pltpu.VMEM((NOUT_PIX, ORDER), F32),
            pltpu.SemaphoreType.DMA((2 * NSEL + 2,)),
        ],
        compiler_params=pltpu.CompilerParams(vmem_limit_bytes=60 << 20),
        name="solve_stamp",
    )(pair_list, ridge, *arrays)


def blend_kernel(n_sky, n_batch, coadd_ref, out_ref, slots, send_sem, recv_sem):
    s = lax.axis_index("sky")
    b = lax.axis_index("batch")
    up = lax.rem(s + 1, n_sky)
    down = lax.rem(s + n_sky - 1, n_sky)
    right = lax.rem(b + 1, n_batch)
    left = lax.rem(b + n_batch - 1, n_batch)
    where = ((down, b), (up, b), (s, left), (s, right))
    barrier = pltpu.get_barrier_semaphore()
    for device in where:
        pl.semaphore_signal(barrier, inc=1, device_id=device, device_id_type=MESH)
    pl.semaphore_wait(barrier, 4)
    copies = [
        pltpu.make_async_remote_copy(
            src_ref=coadd_ref, dst_ref=slots.at[n], send_sem=send_sem.at[n], recv_sem=recv_sem.at[n],
            device_id=where[n], device_id_type=MESH,
        )
        for n in range(4)
    ]
    for copy in copies:
        copy.start()
    pixel = lax.broadcasted_iota(jnp.int32, (1, NOUT_PIX), 1)
    line = pixel // SIDE
    place = pixel - line * SIDE
    edge = SIDE - FADE

    def weight(at, low, first, step, there):
        value = (first + step * (at - low)).astype(F32) / (FADE + 1.0)
        value = jnp.where((at >= low) & (at < low + FADE), value, 0.0)
        return jnp.where(there, value, 0.0)

    weights = (
        weight(place, edge, 1, 1, s < n_sky - 1),
        weight(place, 0, FADE, -1, s > 0),
        weight(line, edge, 1, 1, b < n_batch - 1),
        weight(line, 0, FADE, -1, b > 0),
    )
    shifts = (edge, -edge, edge * SIDE, -edge * SIDE)
    result = coadd_ref[...]
    for n in range(4):
        copies[n].wait_recv()
        other = slots[n]
        shift = shifts[n] % NOUT_PIX
        moved = jnp.concatenate([other[:, NOUT_PIX - shift :], other[:, : NOUT_PIX - shift]], axis=1)
        result = result + weights[n] * moved
    out_ref[...] = result
    for copy in copies:
        copy.wait_send()


def blend(coadd):
    n_sky, n_batch = lax.axis_size("sky"), lax.axis_size("batch")
    return pl.pallas_call(
        functools.partial(blend_kernel, n_sky, n_batch),
        out_shape=jax.ShapeDtypeStruct((LAYERS, NOUT_PIX), F32),
        in_specs=[pl.BlockSpec(memory_space=pltpu.VMEM)],
        out_specs=pl.BlockSpec(memory_space=pltpu.VMEM),
        scratch_shapes=[
            pltpu.VMEM((4, LAYERS, NOUT_PIX), F32),
            pltpu.SemaphoreType.DMA((4,)),
            pltpu.SemaphoreType.DMA((4,)),
        ],
        compiler_params=pltpu.CompilerParams(collective_id=1, has_side_effects=True, vmem_limit_bytes=4 << 20),
        name="blend_edges",
    )(coadd)


def local(features, target, images, layer_mask, pair_list, ridge_weight):
    gathered = gather_window(
        features.reshape(NPIX, FEAT),
        images.reshape(LAYERS, NPIX),
        layer_mask.reshape(LAYERS),
        target.reshape(NOUT_PIX, FEAT),
    )
    transfer, coadd = solve(pair_list.reshape(NSEL), ridge_weight.reshape(1), *gathered)
    final = blend(coadd)
    return (transfer.T.reshape(1, 1, ORDER, NOUT_PIX), final.reshape(LAYERS, SIDE, SIDE))


def solution(mesh):
    in_specs = (
        P("batch", "sky", None, None),
        P("batch", "sky", None, None),
        P("batch", "sky", None, None),
        P("batch", "sky", None),
        P("batch", "sky", None),
        P("batch", "sky"),
    )
    out_specs = (P("batch", "sky", None, None), P(None, "batch", "sky"))
    return jax.shard_map(local, mesh=mesh, in_specs=in_specs, out_specs=out_specs, check_vma=False)
```

```python
import functools

import jax
import jax.numpy as jnp
from jax import lax
from jax.experimental import pallas as pl
from jax.experimental.pallas import tpu as pltpu
from jax.sharding import PartitionSpec as P

NPIX = 80
FEAT = 1024
SIDE = 24
LAYERS = 16
NSEL = 9
FADE = 4
ORDER = 720
NOUT_PIX = 576
CAND = 12

TILE = 128
NBLOCK = 6
PADDED = TILE * NBLOCK
PARTS = (pl.ds(0, 24), pl.ds(24, 16), pl.ds(40, 24), pl.ds(64, 16))
MESH = pl.DeviceIdType.MESH
HIGH = lax.Precision.HIGH
NT = (((1,), (1,)), ((), ()))
F32 = jnp.float32
BF16 = jnp.bfloat16


def halves(x):
    top = x.astype(BF16)
    return top, (x - top.astype(F32)).astype(BF16)


def gather_kernel(
    n_sky, n_batch, feat_ref, image_ref, mask_ref, target_ref, top_ref, low_ref, stamps_ref, target_top_ref, target_low_ref,
    window, target, masked, top, low, target_top, target_low, local_sem, out_sem, fs_sem, fr_sem, ys_sem, yr_sem, is_sem, ir_sem, js_sem, jr_sem,
):
    s = lax.axis_index("sky")
    b = lax.axis_index("batch")
    up = lax.rem(s + 1, n_sky)
    down = lax.rem(s + n_sky - 1, n_sky)
    right = lax.rem(b + 1, n_batch)
    left = lax.rem(b + n_batch - 1, n_batch)
    far = lax.rem(b + 2, n_batch)

    barrier = pltpu.get_barrier_semaphore()
    for where in ((s, left), (s, right), (up, b), (down, b)):
        pl.semaphore_signal(barrier, inc=1, device_id=where, device_id_type=MESH)
    fetch_target = pltpu.make_async_copy(target_ref, target, local_sem.at[0])
    fetch_target.start()
    fetch_own = pltpu.make_async_copy(feat_ref, window.at[3 * b + 1], local_sem.at[1])
    fetch_own.start()

    row = lax.broadcasted_iota(jnp.int32, (LAYERS, NPIX), 0)
    keep = jnp.zeros((LAYERS, NPIX), jnp.int32)
    for layer in range(LAYERS):
        keep = jnp.where(row == layer, mask_ref[layer], keep)
    masked[...] = jnp.zeros((LAYERS, TILE), F32)
    masked[:, :NPIX] = image_ref[...] * keep.astype(F32)

    pl.semaphore_wait(barrier, 4)

    def remote(src, dst, send, recv, where):
        return pltpu.make_async_remote_copy(
            src_ref=src, dst_ref=dst, send_sem=send, recv_sem=recv, device_id=where, device_id_type=MESH
        )

    def along(direction, number, owner, part, src=None):
        slot = window.at[3 * owner + 1, PARTS[part]]
        where = (s, left) if direction else (s, right)
        return remote(
            slot if src is None else src, slot, fs_sem.at[direction, number], fr_sem.at[direction, number], where
        )

    def across(place, owner, part, src=None):
        base = window.at[3 * owner + 1, PARTS[part]] if src is None else src
        number = 4 * place + part
        return (
            remote(base, window.at[3 * owner, PARTS[part]], ys_sem.at[0, number], yr_sem.at[0, number], (up, b)),
            remote(base, window.at[3 * owner + 2, PARTS[part]], ys_sem.at[1, number], yr_sem.at[1, number], (down, b)),
        )

    def image_along(number, owner, where, src):
        return remote(src, stamps_ref.at[3 * owner + 1], is_sem.at[number], ir_sem.at[number], where)

    def image_across(place, owner, src):
        return (
            remote(src, stamps_ref.at[3 * owner], js_sem.at[0, place], jr_sem.at[0, place], (up, b)),
            remote(src, stamps_ref.at[3 * owner + 2], js_sem.at[1, place], jr_sem.at[1, place], (down, b)),
        )

    sends = []

    def start(*copies):
        for copy in copies:
            copy.start()
        sends.extend(copies)

    start(image_along(0, b, (s, right), masked), image_along(1, b, (s, left), masked))
    for part in range(4):
        own = feat_ref.at[PARTS[part]]
        start(along(0, part, b, part, own), along(1, part, b, 3 - part, feat_ref.at[PARTS[3 - part]]))
        start(*across(0, b, part, own))
    start(*image_across(0, b, masked))
    stamps_ref[3 * b + 1] = masked[...]

    def convert(slot, part, values, blank=None):
        if blank is not None:
            values = jnp.where(blank, 0.0, values)
        rows = PARTS[part]
        top[slot, rows, :], low[slot, rows, :] = halves(values)

    leaving = []

    def leave(source, out, sem):
        copy = pltpu.make_async_copy(source, out, sem)
        copy.start()
        leaving.append(copy)

    def ship(slot, number):
        leave(top.at[slot], top_ref.at[slot], out_sem.at[0, number])
        leave(low.at[slot], low_ref.at[slot], out_sem.at[1, number])

    def settle(place, owner):
        for part in range(4):
            for copy in across(place, owner, part):
                copy.wait_recv()
            convert(3 * owner, part, window[3 * owner, PARTS[part], :], s == 0)
            convert(3 * owner + 2, part, window[3 * owner + 2, PARTS[part], :], s == n_sky - 1)
        ship(3 * owner, 3 * place)
        ship(3 * owner + 2, 3 * place + 2)
        for copy in image_across(place, owner, masked):
            copy.wait_recv()
        stamps_ref[3 * owner] = jnp.where(s == 0, 0.0, stamps_ref[3 * owner])
        stamps_ref[3 * owner + 2] = jnp.where(s == n_sky - 1, 0.0, stamps_ref[3 * owner + 2])

    for part in (0, 1):
        along(0, part, left, part).wait_recv()
        start(along(0, 4 + part, left, part))
        start(*across(1, left, part))
        along(1, part, right, 3 - part).wait_recv()
        start(along(1, 4 + part, right, 3 - part))
        start(*across(2, right, 3 - part))
    image_along(0, left, (s, left), masked).wait_recv()
    start(image_along(2, left, (s, right), stamps_ref.at[3 * left + 1]))
    start(*image_across(1, left, stamps_ref.at[3 * left + 1]))
    image_along(1, right, (s, right), masked).wait_recv()
    start(*image_across(2, right, stamps_ref.at[3 * right + 1]))
    fetch_own.wait()
    for part in range(4):
        convert(3 * b + 1, part, window[3 * b + 1, PARTS[part], :])
    ship(3 * b + 1, 1)
    for part in (2, 3):
        along(0, part, left, part).wait_recv()
        start(*across(1, left, part))
        along(1, part, right, 3 - part).wait_recv()
        start(*across(2, right, 3 - part))
    image_along(2, far, (s, left), masked).wait_recv()
    start(*image_across(3, far, stamps_ref.at[3 * far + 1]))
    fetch_target.wait()
    target_top[...], target_low[...] = halves(target[...])
    leave(target_top, target_top_ref, out_sem.at[0, CAND])
    leave(target_low, target_low_ref, out_sem.at[1, CAND])
    for part in (0, 1):
        along(0, 4 + part, far, part).wait_recv()
        start(*across(3, far, part))
        along(1, 4 + part, far, 3 - part).wait_recv()
        start(*across(3, far, 3 - part))
    for place, owner in enumerate((left, right, far)):
        for part in range(4):
            convert(3 * owner + 1, part, window[3 * owner + 1, PARTS[part], :])
        ship(3 * owner + 1, 3 * place + 4)
    for place, owner in enumerate((b, left, right, far)):
        settle(place, owner)
    for copy in sends:
        copy.wait_send()
    for copy in leaving:
        copy.wait()


def gather_window(features, images, layer_mask, target):
    n_sky, n_batch = lax.axis_size("sky"), lax.axis_size("batch")
    vmem, hbm = pl.BlockSpec(memory_space=pltpu.VMEM), pl.BlockSpec(memory_space=pltpu.HBM)
    return pl.pallas_call(
        functools.partial(gather_kernel, n_sky, n_batch),
        out_shape=(
            jax.ShapeDtypeStruct((CAND, NPIX, FEAT), BF16),
            jax.ShapeDtypeStruct((CAND, NPIX, FEAT), BF16),
            jax.ShapeDtypeStruct((CAND, LAYERS, TILE), F32),
            jax.ShapeDtypeStruct((NOUT_PIX, FEAT), BF16),
            jax.ShapeDtypeStruct((NOUT_PIX, FEAT), BF16),
        ),
        in_specs=[
            pl.BlockSpec(memory_space=pltpu.HBM),
            vmem,
            pl.BlockSpec(memory_space=pltpu.SMEM),
            pl.BlockSpec(memory_space=pltpu.HBM),
        ],
        out_specs=(hbm, hbm, vmem, hbm, hbm),
        scratch_shapes=[
            pltpu.VMEM((CAND, NPIX, FEAT), F32),
            pltpu.VMEM((NOUT_PIX, FEAT), F32),
            pltpu.VMEM((LAYERS, TILE), F32),
            pltpu.VMEM((CAND, NPIX, FEAT), BF16),
            pltpu.VMEM((CAND, NPIX, FEAT), BF16),
            pltpu.VMEM((NOUT_PIX, FEAT), BF16),
            pltpu.VMEM((NOUT_PIX, FEAT), BF16),
            pltpu.SemaphoreType.DMA((2,)),
            pltpu.SemaphoreType.DMA((2, CAND + 1)),
            pltpu.SemaphoreType.DMA((2, 6)),
            pltpu.SemaphoreType.DMA((2, 6)),
            pltpu.SemaphoreType.DMA((2, 16)),
            pltpu.SemaphoreType.DMA((2, 16)),
            pltpu.SemaphoreType.DMA((3,)),
            pltpu.SemaphoreType.DMA((3,)),
            pltpu.SemaphoreType.DMA((2, 4)),
            pltpu.SemaphoreType.DMA((2, 4)),
        ],
        compiler_params=pltpu.CompilerParams(
            collective_id=0, has_side_effects=True, vmem_limit_bytes=60 << 20
        ),
        name="gather_window",
    )(features, images, layer_mask, target)


def row_of(tile, index):
    return jnp.broadcast_to(tile[index : index + 1, :], (8, TILE))


def column_of(tile, index):
    return jnp.broadcast_to(tile[:, index : index + 1], (8, TILE))


def total(terms):
    while len(terms) > 1:
        terms = [terms[i] + terms[i + 1] if i + 1 < len(terms) else terms[i] for i in range(0, len(terms), 2)]
    return terms[0]


def reduce_single(block, carried, row):
    block, carried = list(block), list(carried)
    for p in range(8):
        scale = 1.0 / row_of(block[p], p)
        pivot = block[p]
        here = row == p

        def step(tile):
            scaled = row_of(tile, p) * scale
            return jnp.where(here, scaled, tile - pivot * scaled)

        for j in range(p + 1, 8):
            block[j] = step(block[j])
        carried = [step(tile) for tile in carried]
    return carried


def reduce_paired(block, carried, row):
    block, carried = list(block), list(carried)
    for p in range(0, 8, 2):
        q = p + 1
        first, mixed, second = row_of(block[p], p), row_of(block[q], p), row_of(block[q], q)
        scale = 1.0 / (first * second - mixed * mixed)
        upper, cross, lower = second * scale, mixed * scale, first * scale
        pivot_p, pivot_q = block[p], block[q]
        at_p, at_q = row == p, row == q

        def step(tile):
            x, y = row_of(tile, p), row_of(tile, q)
            new_p = upper * x - cross * y
            new_q = lower * y - cross * x
            return jnp.where(at_p, new_p, jnp.where(at_q, new_q, tile - (pivot_p * new_p + pivot_q * new_q)))

        for j in range(q + 1, 8):
            block[j] = step(block[j])
        carried = [step(tile) for tile in carried]
    return carried


def invert_tile(groups, jobs):
    row = lax.broadcasted_iota(jnp.int32, (8, TILE), 0)
    lane = lax.broadcasted_iota(jnp.int32, (8, TILE), 1)
    groups = list(groups)
    count = len(groups)
    zero = jnp.zeros((16, TILE), BF16)
    for k0 in range(0, count, 2):
        k1 = k0 + 1
        in0 = (lane >= 8 * k0) & (lane < 8 * k0 + 8)
        in1 = (lane >= 8 * k1) & (lane < 8 * k1 + 8)
        inside = in0 | in1
        top, low = groups[k0], groups[k1]
        near = [k1 + 1, k1 + 2] if k1 + 2 < count else []
        far = [i for i in range(count) if i not in near and i not in (k0, k1)]
        diag = [column_of(top, 8 * k0 + j) for j in range(8)]
        beside = [column_of(top, 8 * k1 + j) for j in range(8)]
        below = [column_of(low, 8 * k0 + j) for j in range(8)]
        corner = [column_of(low, 8 * k1 + j) for j in range(8)]
        factors = {i: [column_of(groups[i], 8 * k0 + j) for j in range(16)] for i in near}
        for job in jobs[k0 // 2 * len(jobs) * 2 // count : (k0 // 2 + 1) * len(jobs) * 2 // count]:
            job()
        panel = jnp.where(in0, jnp.where(lane - 8 * k0 == row, 1.0, 0.0), top)
        out = reduce_single(diag, beside + [panel], row)
        upper, top = out[:8], out[8]
        corner = [corner[m] - total([below[j] * row_of(upper[m], j) for j in range(8)]) for m in range(8)]
        low = jnp.where(in0, 0.0, low) - total([below[j] * row_of(top, j) for j in range(8)])
        panel = jnp.where(in1, jnp.where(lane - 8 * k1 == row, 1.0, 0.0), low)
        low = reduce_paired(corner, [panel], row)[0]
        low_rows = [row_of(low, j) for j in range(8)]
        top = jnp.where(in1, 0.0, top) - total([upper[j] * low_rows[j] for j in range(8)])
        rows = [row_of(top, j) for j in range(8)] + low_rows
        groups[k0], groups[k1] = top, low
        old = jnp.concatenate([groups[i] for i in far], axis=0)
        for i in near:
            groups[i] = jnp.where(inside, 0.0, groups[i]) - total([factors[i][j] * rows[j] for j in range(16)])
        old_top, old_low = halves(old)
        new_top, new_low = halves(jnp.concatenate([top, low], axis=0))
        before, after = [zero] * (k0 // 2), [zero] * (TILE // 16 - 1 - k0 // 2)
        new_top = jnp.concatenate(before + [new_top] + after, axis=0)
        new_low = jnp.concatenate(before + [new_low] + after, axis=0)
        change = jnp.dot(
            jnp.concatenate([old_top, old_low], axis=1),
            jnp.concatenate([new_top, new_top], axis=0),
            preferred_element_type=F32,
        ) + jnp.dot(old_top, new_low, preferred_element_type=F32)
        for n, i in enumerate(far):
            groups[i] = jnp.where(inside, 0.0, groups[i]) - change[8 * n : 8 * n + 8]
    return groups


def dot(a, b, dims=((1,), (0,))):
    return lax.dot_general(a, b, (dims, ((), ())), precision=HIGH, preferred_element_type=F32)


def solve_kernel(
    pair_ref, ridge_ref, top_ref, low_ref, stamps_ref, target_top_ref, target_low_ref, transfer_ref, coadd_ref,
    feat_top, feat_low, target_top, target_low, system, right,
    left_top, left_low, across_top, across_low, column_top, column_low, right_top, right_low, diag, inverse, previous, result, sem,
):
    copies = []
    for k in range(NSEL):
        rows = pl.ds(NPIX * k, NPIX)
        copies.append(pltpu.make_async_copy(top_ref.at[pair_ref[k]], feat_top.at[rows], sem.at[k]))
        copies.append(pltpu.make_async_copy(low_ref.at[pair_ref[k]], feat_low.at[rows], sem.at[NSEL + k]))
    later = [
        pltpu.make_async_copy(target_top_ref, target_top, sem.at[2 * NSEL]),
        pltpu.make_async_copy(target_low_ref, target_low, sem.at[2 * NSEL + 1]),
    ]
    for copy in copies + later:
        copy.start()
    feat_top[ORDER:, :] = jnp.zeros((PADDED - ORDER, FEAT), BF16)
    feat_low[ORDER:, :] = jnp.zeros((PADDED - ORDER, FEAT), BF16)
    for copy in copies:
        copy.wait()

    def product(a_top, a_low, b_top, b_low):
        result = lax.dot_general(a_top, b_top, NT, preferred_element_type=F32)
        result += lax.dot_general(a_top, b_low, NT, preferred_element_type=F32)
        return result + lax.dot_general(a_low, b_top, NT, preferred_element_type=F32)

    wide = 2 * TILE
    for k in range(PADDED // wide):
        rows, rest = pl.ds(wide * k, wide), pl.ds(wide * k, PADDED - wide * k)
        system[rows, rest] = product(feat_top[rows, :], feat_low[rows, :], feat_top[rest, :], feat_low[rest, :])
    for k in range(PADDED // wide):
        for j in range(k):
            rows, columns = pl.ds(wide * k, wide), pl.ds(wide * j, wide)
            system[rows, columns] = system[columns, rows].T
    ridge = ridge_ref[0]
    eye = jnp.where(
        lax.broadcasted_iota(jnp.int32, (TILE, TILE), 0) == lax.broadcasted_iota(jnp.int32, (TILE, TILE), 1),
        ridge, 0.0,
    )
    for k in range(NBLOCK):
        at = pl.ds(TILE * k, TILE)
        system[at, at] += eye
    diag[...] = system[:TILE, :TILE]

    for copy in later:
        copy.wait()
    third = PADDED // 3
    share = NOUT_PIX // 3

    def block(k):
        return pl.ds(TILE * k, TILE)

    def product_of_halves(a_top, a_low, b_top, b_low):
        result = lax.dot_general(
            jnp.concatenate([a_top, a_low], axis=1), jnp.concatenate([b_top, b_top], axis=1), NT,
            preferred_element_type=F32,
        )
        return result + lax.dot_general(a_top, b_low, NT, preferred_element_type=F32)

    def take_job(j):
        def job():
            at = block(j)
            across_top[...], across_low[...] = halves(system[at, :])
            system[at, :] = jnp.zeros((TILE, PADDED), F32)
            column_top[...], column_low[...] = halves(system[:, at])
        return job

    def left_job(j, part):
        def job():
            rows = pl.ds(third * part, third)
            left = dot(system[rows, block(j)], previous[...])
            left_top[rows, :], left_low[rows, :] = halves(left)
            if third * part <= TILE * j < third * part + third:
                left_top[block(j), :], left_low[block(j), :] = halves(-previous[...])
        return job

    def update_job(j, part):
        def job():
            first = max(third * part, TILE * (j + 1))
            columns = pl.ds(first, third * part + third - first)
            top = across_top[:, columns]
            change = jnp.dot(
                jnp.concatenate([left_top[...], left_low[...]], axis=1),
                jnp.concatenate([top, top], axis=0),
                preferred_element_type=F32,
            )
            change += jnp.dot(left_top[...], across_low[:, columns], preferred_element_type=F32)
            system[:, columns] -= change
        return job

    def scale_job(j):
        def job():
            scaled = dot(right[:, block(j)], previous[...])
            right[:, block(j)] = scaled
            right_top[...], right_low[...] = halves(scaled)
        return job

    def right_update_job(j, part):
        def job():
            columns = pl.ds(third * part, third)
            right[:, columns] -= product_of_halves(
                right_top[...], right_low[...], column_top[columns, :], column_low[columns, :]
            )
        return job

    def invert(rows, jobs):
        groups = invert_tile([diag[8 * i : 8 * i + 8, :] for i in range(rows // 8)], jobs)
        for i, group in enumerate(groups):
            inverse[8 * i : 8 * i + 8, :] = group

    def advance(k):
        at, then = block(k), block(k + 1)
        diag[...] = system[then, then] - dot(dot(system[then, at], inverse[...]), system[at, then])
        previous[...] = inverse[...]

    def jobs_after(j):
        jobs = [take_job(j), scale_job(j)] + [left_job(j, part) for part in range(3)]
        jobs += [update_job(j, part) for part in range(3) if third * part + third > TILE * (j + 1)]
        return jobs + [right_update_job(j, part) for part in range(3)]

    right[...] = product(target_top[...], target_low[...], feat_top[...], feat_low[...])
    invert(TILE, [])
    advance(0)
    for k in range(1, NBLOCK - 1):
        invert(TILE, jobs_after(k - 1))
        advance(k)
    last = NBLOCK - 1
    inverse[...] = jnp.zeros((TILE, TILE), F32)
    invert(ORDER - TILE * last, jobs_after(last - 1))
    column_top[...], column_low[...] = halves(system[:, block(last)])
    outgoing = []
    for part in range(3):
        rows = pl.ds(share * part, share)
        scaled = dot(right[rows, block(last)], inverse[...])
        top, low = halves(scaled)
        head = pl.ds(0, TILE * last)
        right[rows, head] -= product_of_halves(top, low, column_top[head, :], column_low[head, :])
        right[rows, block(last)] = scaled
        result[rows, :] = right[rows, pl.ds(0, ORDER)]
        copy = pltpu.make_async_copy(result.at[rows], transfer_ref.at[rows], sem.at[part])
        copy.start()
        outgoing.append(copy)

    empty = jnp.zeros((LAYERS, TILE), F32)
    strips = [empty] * (NBLOCK + 1)
    for k in range(NSEL):
        first, shift = divmod(NPIX * k, TILE)
        wide = jnp.concatenate([stamps_ref[pair_ref[k]], empty], axis=1)
        if shift:
            wide = pltpu.roll(wide, shift, 1)
        strips[first] = strips[first] + wide[:, :TILE]
        strips[first + 1] = strips[first + 1] + wide[:, TILE:]
    coadd_ref[...] = dot(jnp.concatenate(strips[:NBLOCK], axis=1), right[...], ((1,), (1,)))
    for copy in outgoing:
        copy.wait()


def solve(pair_list, ridge, *arrays):
    return pl.pallas_call(
        solve_kernel,
        out_shape=(
            jax.ShapeDtypeStruct((NOUT_PIX, ORDER), F32),
            jax.ShapeDtypeStruct((LAYERS, NOUT_PIX), F32),
        ),
        in_specs=[
            pl.BlockSpec(memory_space=pltpu.SMEM),
            pl.BlockSpec(memory_space=pltpu.SMEM),
            pl.BlockSpec(memory_space=pltpu.HBM),
            pl.BlockSpec(memory_space=pltpu.HBM),
            pl.BlockSpec(memory_space=pltpu.VMEM),
            pl.BlockSpec(memory_space=pltpu.HBM),
            pl.BlockSpec(memory_space=pltpu.HBM),
        ],
        out_specs=(pl.BlockSpec(memory_space=pltpu.HBM), pl.BlockSpec(memory_space=pltpu.VMEM)),
        scratch_shapes=[
            pltpu.VMEM((PADDED, FEAT), BF16),
            pltpu.VMEM((PADDED, FEAT), BF16),
            pltpu.VMEM((NOUT_PIX, FEAT), BF16),
            pltpu.VMEM((NOUT_PIX, FEAT), BF16),
            pltpu.VMEM((PADDED, PADDED), F32),
            pltpu.VMEM((NOUT_PIX, PADDED), F32),
            pltpu.VMEM((PADDED, TILE), BF16),
            pltpu.VMEM((PADDED, TILE), BF16),
            pltpu.VMEM((TILE, PADDED), BF16),
            pltpu.VMEM((TILE, PADDED), BF16),
            pltpu.VMEM((PADDED, TILE), BF16),
            pltpu.VMEM((PADDED, TILE), BF16),
            pltpu.VMEM((NOUT_PIX, TILE), BF16),
            pltpu.VMEM((NOUT_PIX, TILE), BF16),
            pltpu.VMEM((TILE, TILE), F32),
            pltpu.VMEM((TILE, TILE), F32),
            pltpu.VMEM((TILE, TILE), F32),
            pltpu.VMEM((NOUT_PIX, ORDER), F32),
            pltpu.SemaphoreType.DMA((2 * NSEL + 2,)),
        ],
        compiler_params=pltpu.CompilerParams(vmem_limit_bytes=60 << 20),
        name="solve_stamp",
    )(pair_list, ridge, *arrays)


def blend_kernel(n_sky, n_batch, coadd_ref, out_ref, slots, send_sem, recv_sem):
    s = lax.axis_index("sky")
    b = lax.axis_index("batch")
    up = lax.rem(s + 1, n_sky)
    down = lax.rem(s + n_sky - 1, n_sky)
    right = lax.rem(b + 1, n_batch)
    left = lax.rem(b + n_batch - 1, n_batch)
    where = ((down, b), (up, b), (s, left), (s, right))
    barrier = pltpu.get_barrier_semaphore()
    for device in where:
        pl.semaphore_signal(barrier, inc=1, device_id=device, device_id_type=MESH)
    pl.semaphore_wait(barrier, 4)
    copies = [
        pltpu.make_async_remote_copy(
            src_ref=coadd_ref, dst_ref=slots.at[n], send_sem=send_sem.at[n], recv_sem=recv_sem.at[n],
            device_id=where[n], device_id_type=MESH,
        )
        for n in range(4)
    ]
    for copy in copies:
        copy.start()
    pixel = lax.broadcasted_iota(jnp.int32, (1, NOUT_PIX), 1)
    line = pixel // SIDE
    place = pixel - line * SIDE
    edge = SIDE - FADE

    def weight(at, low, first, step, there):
        value = (first + step * (at - low)).astype(F32) / (FADE + 1.0)
        value = jnp.where((at >= low) & (at < low + FADE), value, 0.0)
        return jnp.where(there, value, 0.0)

    weights = (
        weight(place, edge, 1, 1, s < n_sky - 1),
        weight(place, 0, FADE, -1, s > 0),
        weight(line, edge, 1, 1, b < n_batch - 1),
        weight(line, 0, FADE, -1, b > 0),
    )
    shifts = (edge, -edge, edge * SIDE, -edge * SIDE)
    result = coadd_ref[...]
    for n in range(4):
        copies[n].wait_recv()
        other = slots[n]
        shift = shifts[n] % NOUT_PIX
        moved = jnp.concatenate([other[:, NOUT_PIX - shift :], other[:, : NOUT_PIX - shift]], axis=1)
        result = result + weights[n] * moved
    out_ref[...] = result
    for copy in copies:
        copy.wait_send()


def blend(coadd):
    n_sky, n_batch = lax.axis_size("sky"), lax.axis_size("batch")
    return pl.pallas_call(
        functools.partial(blend_kernel, n_sky, n_batch),
        out_shape=jax.ShapeDtypeStruct((LAYERS, NOUT_PIX), F32),
        in_specs=[pl.BlockSpec(memory_space=pltpu.VMEM)],
        out_specs=pl.BlockSpec(memory_space=pltpu.VMEM),
        scratch_shapes=[
            pltpu.VMEM((4, LAYERS, NOUT_PIX), F32),
            pltpu.SemaphoreType.DMA((4,)),
            pltpu.SemaphoreType.DMA((4,)),
        ],
        compiler_params=pltpu.CompilerParams(collective_id=1, has_side_effects=True, vmem_limit_bytes=4 << 20),
        name="blend_edges",
    )(coadd)


def local(features, target, images, layer_mask, pair_list, ridge_weight):
    gathered = gather_window(
        features.reshape(NPIX, FEAT),
        images.reshape(LAYERS, NPIX),
        layer_mask.reshape(LAYERS),
        target.reshape(NOUT_PIX, FEAT),
    )
    transfer, coadd = solve(pair_list.reshape(NSEL), ridge_weight.reshape(1), *gathered)
    final = blend(coadd)
    return (transfer.T.reshape(1, 1, ORDER, NOUT_PIX), final.reshape(LAYERS, SIDE, SIDE))


def solution(mesh):
    in_specs = (
        P("batch", "sky", None, None),
        P("batch", "sky", None, None),
        P("batch", "sky", None, None),
        P("batch", "sky", None),
        P("batch", "sky", None),
        P("batch", "sky"),
    )
    out_specs = (P("batch", "sky", None, None), P(None, "batch", "sky"))
    return jax.shard_map(local, mesh=mesh, in_specs=in_specs, out_specs=out_specs, check_vma=False)
```

```python
import functools

import jax
import jax.numpy as jnp
from jax import lax
from jax.experimental import pallas as pl
from jax.experimental.pallas import tpu as pltpu
from jax.sharding import PartitionSpec as P

NPIX = 80
FEAT = 1024
SIDE = 24
LAYERS = 16
NSEL = 9
FADE = 4
ORDER = 720
NOUT_PIX = 576
CAND = 12

TILE = 128
NBLOCK = 6
PADDED = TILE * NBLOCK
PARTS = (pl.ds(0, 40), pl.ds(40, 40))
MESH = pl.DeviceIdType.MESH
HIGH = lax.Precision.HIGH
NT = (((1,), (1,)), ((), ()))
F32 = jnp.float32
BF16 = jnp.bfloat16


def halves(x):
    top = x.astype(BF16)
    return top, (x - top.astype(F32)).astype(BF16)


def gather_kernel(
    n_sky, n_batch, feat_ref, image_ref, mask_ref, target_ref, top_ref, low_ref, stamps_ref, target_top_ref, target_low_ref,
    window, target, masked, top, low, target_top, target_low, local_sem, out_sem, fs_sem, fr_sem, ys_sem, yr_sem, is_sem, ir_sem, js_sem, jr_sem,
):
    s = lax.axis_index("sky")
    b = lax.axis_index("batch")
    up = lax.rem(s + 1, n_sky)
    down = lax.rem(s + n_sky - 1, n_sky)
    right = lax.rem(b + 1, n_batch)
    left = lax.rem(b + n_batch - 1, n_batch)
    far = lax.rem(b + 2, n_batch)

    barrier = pltpu.get_barrier_semaphore()
    for where in ((s, left), (s, right), (up, b), (down, b)):
        pl.semaphore_signal(barrier, inc=1, device_id=where, device_id_type=MESH)
    fetch_target = pltpu.make_async_copy(target_ref, target, local_sem.at[0])
    fetch_target.start()
    fetch_own = pltpu.make_async_copy(feat_ref, window.at[3 * b + 1], local_sem.at[1])
    fetch_own.start()

    row = lax.broadcasted_iota(jnp.int32, (LAYERS, NPIX), 0)
    keep = jnp.zeros((LAYERS, NPIX), jnp.int32)
    for layer in range(LAYERS):
        keep = jnp.where(row == layer, mask_ref[layer], keep)
    masked[...] = jnp.zeros((LAYERS, TILE), F32)
    masked[:, :NPIX] = image_ref[...] * keep.astype(F32)

    pl.semaphore_wait(barrier, 4)

    def remote(src, dst, send, recv, where):
        return pltpu.make_async_remote_copy(
            src_ref=src, dst_ref=dst, send_sem=send, recv_sem=recv, device_id=where, device_id_type=MESH
        )

    def along(direction, number, owner, part, src=None):
        slot = window.at[3 * owner + 1, PARTS[part]]
        where = (s, left) if direction else (s, right)
        return remote(
            slot if src is None else src, slot, fs_sem.at[direction, number], fr_sem.at[direction, number], where
        )

    def across(place, owner, part, src=None):
        base = window.at[3 * owner + 1, PARTS[part]] if src is None else src
        number = 2 * place + part
        return (
            remote(base, window.at[3 * owner, PARTS[part]], ys_sem.at[0, number], yr_sem.at[0, number], (up, b)),
            remote(base, window.at[3 * owner + 2, PARTS[part]], ys_sem.at[1, number], yr_sem.at[1, number], (down, b)),
        )

    def image_along(number, owner, where, src):
        return remote(src, stamps_ref.at[3 * owner + 1], is_sem.at[number], ir_sem.at[number], where)

    def image_across(place, owner, src):
        return (
            remote(src, stamps_ref.at[3 * owner], js_sem.at[0, place], jr_sem.at[0, place], (up, b)),
            remote(src, stamps_ref.at[3 * owner + 2], js_sem.at[1, place], jr_sem.at[1, place], (down, b)),
        )

    sends = []

    def start(*copies):
        for copy in copies:
            copy.start()
        sends.extend(copies)

    start(image_along(0, b, (s, right), masked), image_along(1, b, (s, left), masked))
    for part in range(2):
        own = feat_ref.at[PARTS[part]]
        start(along(0, part, b, part, own), along(1, part, b, 1 - part, feat_ref.at[PARTS[1 - part]]))
        start(*across(0, b, part, own))
    start(*image_across(0, b, masked))
    stamps_ref[3 * b + 1] = masked[...]

    def convert(slot, blank=None):
        values = window[slot]
        if blank is not None:
            values = jnp.where(blank, 0.0, values)
        top[slot], low[slot] = halves(values)

    leaving = []

    def leave(source, out, sem):
        copy = pltpu.make_async_copy(source, out, sem)
        copy.start()
        leaving.append(copy)

    def ship(slot, number):
        leave(top.at[slot], top_ref.at[slot], out_sem.at[0, number])
        leave(low.at[slot], low_ref.at[slot], out_sem.at[1, number])

    def settle(place, owner):
        for part in range(2):
            for copy in across(place, owner, part):
                copy.wait_recv()
        convert(3 * owner, s == 0)
        convert(3 * owner + 2, s == n_sky - 1)
        ship(3 * owner, 3 * place)
        ship(3 * owner + 2, 3 * place + 2)
        for copy in image_across(place, owner, masked):
            copy.wait_recv()
        stamps_ref[3 * owner] = jnp.where(s == 0, 0.0, stamps_ref[3 * owner])
        stamps_ref[3 * owner + 2] = jnp.where(s == n_sky - 1, 0.0, stamps_ref[3 * owner + 2])

    for part in (0,):
        along(0, part, left, part).wait_recv()
        start(along(0, 2 + part, left, part))
        start(*across(1, left, part))
        along(1, part, right, 1 - part).wait_recv()
        start(along(1, 2 + part, right, 1 - part))
        start(*across(2, right, 1 - part))
    image_along(0, left, (s, left), masked).wait_recv()
    start(image_along(2, left, (s, right), stamps_ref.at[3 * left + 1]))
    start(*image_across(1, left, stamps_ref.at[3 * left + 1]))
    image_along(1, right, (s, right), masked).wait_recv()
    start(*image_across(2, right, stamps_ref.at[3 * right + 1]))
    fetch_own.wait()
    convert(3 * b + 1)
    ship(3 * b + 1, 1)
    for part in (1,):
        along(0, part, left, part).wait_recv()
        start(*across(1, left, part))
        along(1, part, right, 1 - part).wait_recv()
        start(*across(2, right, 1 - part))
    image_along(2, far, (s, left), masked).wait_recv()
    start(*image_across(3, far, stamps_ref.at[3 * far + 1]))
    fetch_target.wait()
    target_top[...], target_low[...] = halves(target[...])
    leave(target_top, target_top_ref, out_sem.at[0, CAND])
    leave(target_low, target_low_ref, out_sem.at[1, CAND])
    for part in (0,):
        along(0, 2 + part, far, part).wait_recv()
        start(*across(3, far, part))
        along(1, 2 + part, far, 1 - part).wait_recv()
        start(*across(3, far, 1 - part))
    for place, owner in enumerate((left, right, far)):
        convert(3 * owner + 1)
        ship(3 * owner + 1, 3 * place + 4)
    for place, owner in enumerate((b, left, right, far)):
        settle(place, owner)
    for copy in sends:
        copy.wait_send()
    for copy in leaving:
        copy.wait()


def gather_window(features, images, layer_mask, target):
    n_sky, n_batch = lax.axis_size("sky"), lax.axis_size("batch")
    vmem, hbm = pl.BlockSpec(memory_space=pltpu.VMEM), pl.BlockSpec(memory_space=pltpu.HBM)
    return pl.pallas_call(
        functools.partial(gather_kernel, n_sky, n_batch),
        out_shape=(
            jax.ShapeDtypeStruct((CAND, NPIX, FEAT), BF16),
            jax.ShapeDtypeStruct((CAND, NPIX, FEAT), BF16),
            jax.ShapeDtypeStruct((CAND, LAYERS, TILE), F32),
            jax.ShapeDtypeStruct((NOUT_PIX, FEAT), BF16),
            jax.ShapeDtypeStruct((NOUT_PIX, FEAT), BF16),
        ),
        in_specs=[
            pl.BlockSpec(memory_space=pltpu.HBM),
            vmem,
            pl.BlockSpec(memory_space=pltpu.SMEM),
            pl.BlockSpec(memory_space=pltpu.HBM),
        ],
        out_specs=(hbm, hbm, vmem, hbm, hbm),
        scratch_shapes=[
            pltpu.VMEM((CAND, NPIX, FEAT), F32),
            pltpu.VMEM((NOUT_PIX, FEAT), F32),
            pltpu.VMEM((LAYERS, TILE), F32),
            pltpu.VMEM((CAND, NPIX, FEAT), BF16),
            pltpu.VMEM((CAND, NPIX, FEAT), BF16),
            pltpu.VMEM((NOUT_PIX, FEAT), BF16),
            pltpu.VMEM((NOUT_PIX, FEAT), BF16),
            pltpu.SemaphoreType.DMA((2,)),
            pltpu.SemaphoreType.DMA((2, CAND + 1)),
            pltpu.SemaphoreType.DMA((2, 3)),
            pltpu.SemaphoreType.DMA((2, 3)),
            pltpu.SemaphoreType.DMA((2, 8)),
            pltpu.SemaphoreType.DMA((2, 8)),
            pltpu.SemaphoreType.DMA((3,)),
            pltpu.SemaphoreType.DMA((3,)),
            pltpu.SemaphoreType.DMA((2, 4)),
            pltpu.SemaphoreType.DMA((2, 4)),
        ],
        compiler_params=pltpu.CompilerParams(
            collective_id=0, has_side_effects=True, vmem_limit_bytes=60 << 20
        ),
        name="gather_window",
    )(features, images, layer_mask, target)


def row_of(tile, index):
    return jnp.broadcast_to(tile[index : index + 1, :], (8, TILE))


def column_of(tile, index):
    return jnp.broadcast_to(tile[:, index : index + 1], (8, TILE))


def total(terms):
    while len(terms) > 1:
        terms = [terms[i] + terms[i + 1] if i + 1 < len(terms) else terms[i] for i in range(0, len(terms), 2)]
    return terms[0]


def reduce_single(block, carried, row):
    block, carried = list(block), list(carried)
    for p in range(8):
        scale = 1.0 / row_of(block[p], p)
        pivot = block[p]
        here = row == p

        def step(tile):
            scaled = row_of(tile, p) * scale
            return jnp.where(here, scaled, tile - pivot * scaled)

        for j in range(p + 1, 8):
            block[j] = step(block[j])
        carried = [step(tile) for tile in carried]
    return carried


def reduce_paired(block, carried, row):
    block, carried = list(block), list(carried)
    for p in range(0, 8, 2):
        q = p + 1
        first, mixed, second = row_of(block[p], p), row_of(block[q], p), row_of(block[q], q)
        scale = 1.0 / (first * second - mixed * mixed)
        upper, cross, lower = second * scale, mixed * scale, first * scale
        pivot_p, pivot_q = block[p], block[q]
        at_p, at_q = row == p, row == q

        def step(tile):
            x, y = row_of(tile, p), row_of(tile, q)
            new_p = upper * x - cross * y
            new_q = lower * y - cross * x
            return jnp.where(at_p, new_p, jnp.where(at_q, new_q, tile - (pivot_p * new_p + pivot_q * new_q)))

        for j in range(q + 1, 8):
            block[j] = step(block[j])
        carried = [step(tile) for tile in carried]
    return carried


def invert_tile(groups, jobs):
    row = lax.broadcasted_iota(jnp.int32, (8, TILE), 0)
    lane = lax.broadcasted_iota(jnp.int32, (8, TILE), 1)
    groups = list(groups)
    count = len(groups)
    zero = jnp.zeros((16, TILE), BF16)
    for k0 in range(0, count, 2):
        k1 = k0 + 1
        in0 = (lane >= 8 * k0) & (lane < 8 * k0 + 8)
        in1 = (lane >= 8 * k1) & (lane < 8 * k1 + 8)
        inside = in0 | in1
        top, low = groups[k0], groups[k1]
        near = [k1 + 1, k1 + 2] if k1 + 2 < count else []
        far = [i for i in range(count) if i not in near and i not in (k0, k1)]
        diag = [column_of(top, 8 * k0 + j) for j in range(8)]
        beside = [column_of(top, 8 * k1 + j) for j in range(8)]
        below = [column_of(low, 8 * k0 + j) for j in range(8)]
        corner = [column_of(low, 8 * k1 + j) for j in range(8)]
        factors = {i: [column_of(groups[i], 8 * k0 + j) for j in range(16)] for i in near}
        for job in jobs[k0 // 2 * len(jobs) * 2 // count : (k0 // 2 + 1) * len(jobs) * 2 // count]:
            job()
        panel = jnp.where(in0, jnp.where(lane - 8 * k0 == row, 1.0, 0.0), top)
        out = reduce_single(diag, beside + [panel], row)
        upper, top = out[:8], out[8]
        corner = [corner[m] - total([below[j] * row_of(upper[m], j) for j in range(8)]) for m in range(8)]
        low = jnp.where(in0, 0.0, low) - total([below[j] * row_of(top, j) for j in range(8)])
        panel = jnp.where(in1, jnp.where(lane - 8 * k1 == row, 1.0, 0.0), low)
        low = reduce_paired(corner, [panel], row)[0]
        low_rows = [row_of(low, j) for j in range(8)]
        top = jnp.where(in1, 0.0, top) - total([upper[j] * low_rows[j] for j in range(8)])
        rows = [row_of(top, j) for j in range(8)] + low_rows
        groups[k0], groups[k1] = top, low
        old = jnp.concatenate([groups[i] for i in far], axis=0)
        for i in near:
            groups[i] = jnp.where(inside, 0.0, groups[i]) - total([factors[i][j] * rows[j] for j in range(16)])
        old_top, old_low = halves(old)
        new_top, new_low = halves(jnp.concatenate([top, low], axis=0))
        before, after = [zero] * (k0 // 2), [zero] * (TILE // 16 - 1 - k0 // 2)
        new_top = jnp.concatenate(before + [new_top] + after, axis=0)
        new_low = jnp.concatenate(before + [new_low] + after, axis=0)
        change = jnp.dot(
            jnp.concatenate([old_top, old_low], axis=1),
            jnp.concatenate([new_top, new_top], axis=0),
            preferred_element_type=F32,
        ) + jnp.dot(old_top, new_low, preferred_element_type=F32)
        for n, i in enumerate(far):
            groups[i] = jnp.where(inside, 0.0, groups[i]) - change[8 * n : 8 * n + 8]
    return groups


def dot(a, b, dims=((1,), (0,))):
    return lax.dot_general(a, b, (dims, ((), ())), precision=HIGH, preferred_element_type=F32)


def solve_kernel(
    pair_ref, ridge_ref, top_ref, low_ref, stamps_ref, target_top_ref, target_low_ref, transfer_ref, coadd_ref,
    feat_top, feat_low, target_top, target_low, system, right,
    left_top, left_low, across_top, across_low, column_top, column_low, right_top, right_low, diag, inverse, previous, result, sem,
):
    copies = []
    for k in range(NSEL):
        rows = pl.ds(NPIX * k, NPIX)
        copies.append(pltpu.make_async_copy(top_ref.at[pair_ref[k]], feat_top.at[rows], sem.at[k]))
        copies.append(pltpu.make_async_copy(low_ref.at[pair_ref[k]], feat_low.at[rows], sem.at[NSEL + k]))
    later = [
        pltpu.make_async_copy(target_top_ref, target_top, sem.at[2 * NSEL]),
        pltpu.make_async_copy(target_low_ref, target_low, sem.at[2 * NSEL + 1]),
    ]
    for copy in copies + later:
        copy.start()
    feat_top[ORDER:, :] = jnp.zeros((PADDED - ORDER, FEAT), BF16)
    feat_low[ORDER:, :] = jnp.zeros((PADDED - ORDER, FEAT), BF16)
    for copy in copies:
        copy.wait()

    def product(a_top, a_low, b_top, b_low):
        result = lax.dot_general(a_top, b_top, NT, preferred_element_type=F32)
        result += lax.dot_general(a_top, b_low, NT, preferred_element_type=F32)
        return result + lax.dot_general(a_low, b_top, NT, preferred_element_type=F32)

    wide = 2 * TILE
    for k in range(PADDED // wide):
        rows, rest = pl.ds(wide * k, wide), pl.ds(wide * k, PADDED - wide * k)
        system[rows, rest] = product(feat_top[rows, :], feat_low[rows, :], feat_top[rest, :], feat_low[rest, :])
    for k in range(PADDED // wide):
        for j in range(k):
            rows, columns = pl.ds(wide * k, wide), pl.ds(wide * j, wide)
            system[rows, columns] = system[columns, rows].T
    ridge = ridge_ref[0]
    eye = jnp.where(
        lax.broadcasted_iota(jnp.int32, (TILE, TILE), 0) == lax.broadcasted_iota(jnp.int32, (TILE, TILE), 1),
        ridge, 0.0,
    )
    for k in range(NBLOCK):
        at = pl.ds(TILE * k, TILE)
        system[at, at] += eye
    diag[...] = system[:TILE, :TILE]

    for copy in later:
        copy.wait()
    third = PADDED // 3
    share = NOUT_PIX // 3

    def block(k):
        return pl.ds(TILE * k, TILE)

    def product_of_halves(a_top, a_low, b_top, b_low):
        result = lax.dot_general(
            jnp.concatenate([a_top, a_low], axis=1), jnp.concatenate([b_top, b_top], axis=1), NT,
            preferred_element_type=F32,
        )
        return result + lax.dot_general(a_top, b_low, NT, preferred_element_type=F32)

    def take_job(j):
        def job():
            at = block(j)
            across_top[...], across_low[...] = halves(system[at, :])
            system[at, :] = jnp.zeros((TILE, PADDED), F32)
            column_top[...], column_low[...] = halves(system[:, at])
        return job

    def left_job(j, part):
        def job():
            rows = pl.ds(third * part, third)
            left = dot(system[rows, block(j)], previous[...])
            left_top[rows, :], left_low[rows, :] = halves(left)
            if third * part <= TILE * j < third * part + third:
                left_top[block(j), :], left_low[block(j), :] = halves(-previous[...])
        return job

    def update_job(j, part):
        def job():
            first = max(third * part, TILE * (j + 1))
            columns = pl.ds(first, third * part + third - first)
            top = across_top[:, columns]
            change = jnp.dot(
                jnp.concatenate([left_top[...], left_low[...]], axis=1),
                jnp.concatenate([top, top], axis=0),
                preferred_element_type=F32,
            )
            change += jnp.dot(left_top[...], across_low[:, columns], preferred_element_type=F32)
            system[:, columns] -= change
        return job

    def scale_job(j):
        def job():
            scaled = dot(right[:, block(j)], previous[...])
            right[:, block(j)] = scaled
            right_top[...], right_low[...] = halves(scaled)
        return job

    def right_update_job(j, part):
        def job():
            columns = pl.ds(third * part, third)
            right[:, columns] -= product_of_halves(
                right_top[...], right_low[...], column_top[columns, :], column_low[columns, :]
            )
        return job

    def invert(rows, jobs):
        groups = invert_tile([diag[8 * i : 8 * i + 8, :] for i in range(rows // 8)], jobs)
        for i, group in enumerate(groups):
            inverse[8 * i : 8 * i + 8, :] = group

    def advance(k):
        at, then = block(k), block(k + 1)
        diag[...] = system[then, then] - dot(dot(system[then, at], inverse[...]), system[at, then])
        previous[...] = inverse[...]

    def jobs_after(j):
        jobs = [take_job(j), scale_job(j)] + [left_job(j, part) for part in range(3)]
        jobs += [update_job(j, part) for part in range(3) if third * part + third > TILE * (j + 1)]
        return jobs + [right_update_job(j, part) for part in range(3)]

    right[...] = product(target_top[...], target_low[...], feat_top[...], feat_low[...])
    invert(TILE, [])
    advance(0)
    for k in range(1, NBLOCK - 1):
        invert(TILE, jobs_after(k - 1))
        advance(k)
    last = NBLOCK - 1
    inverse[...] = jnp.zeros((TILE, TILE), F32)
    invert(ORDER - TILE * last, jobs_after(last - 1))
    column_top[...], column_low[...] = halves(system[:, block(last)])
    outgoing = []
    for part in range(3):
        rows = pl.ds(share * part, share)
        scaled = dot(right[rows, block(last)], inverse[...])
        top, low = halves(scaled)
        head = pl.ds(0, TILE * last)
        right[rows, head] -= product_of_halves(top, low, column_top[head, :], column_low[head, :])
        right[rows, block(last)] = scaled
        result[rows, :] = right[rows, pl.ds(0, ORDER)]
        copy = pltpu.make_async_copy(result.at[rows], transfer_ref.at[rows], sem.at[part])
        copy.start()
        outgoing.append(copy)

    empty = jnp.zeros((LAYERS, TILE), F32)
    strips = [empty] * (NBLOCK + 1)
    for k in range(NSEL):
        first, shift = divmod(NPIX * k, TILE)
        wide = jnp.concatenate([stamps_ref[pair_ref[k]], empty], axis=1)
        if shift:
            wide = pltpu.roll(wide, shift, 1)
        strips[first] = strips[first] + wide[:, :TILE]
        strips[first + 1] = strips[first + 1] + wide[:, TILE:]
    coadd_ref[...] = dot(jnp.concatenate(strips[:NBLOCK], axis=1), right[...], ((1,), (1,)))
    for copy in outgoing:
        copy.wait()


def solve(pair_list, ridge, *arrays):
    return pl.pallas_call(
        solve_kernel,
        out_shape=(
            jax.ShapeDtypeStruct((NOUT_PIX, ORDER), F32),
            jax.ShapeDtypeStruct((LAYERS, NOUT_PIX), F32),
        ),
        in_specs=[
            pl.BlockSpec(memory_space=pltpu.SMEM),
            pl.BlockSpec(memory_space=pltpu.SMEM),
            pl.BlockSpec(memory_space=pltpu.HBM),
            pl.BlockSpec(memory_space=pltpu.HBM),
            pl.BlockSpec(memory_space=pltpu.VMEM),
            pl.BlockSpec(memory_space=pltpu.HBM),
            pl.BlockSpec(memory_space=pltpu.HBM),
        ],
        out_specs=(pl.BlockSpec(memory_space=pltpu.HBM), pl.BlockSpec(memory_space=pltpu.VMEM)),
        scratch_shapes=[
            pltpu.VMEM((PADDED, FEAT), BF16),
            pltpu.VMEM((PADDED, FEAT), BF16),
            pltpu.VMEM((NOUT_PIX, FEAT), BF16),
            pltpu.VMEM((NOUT_PIX, FEAT), BF16),
            pltpu.VMEM((PADDED, PADDED), F32),
            pltpu.VMEM((NOUT_PIX, PADDED), F32),
            pltpu.VMEM((PADDED, TILE), BF16),
            pltpu.VMEM((PADDED, TILE), BF16),
            pltpu.VMEM((TILE, PADDED), BF16),
            pltpu.VMEM((TILE, PADDED), BF16),
            pltpu.VMEM((PADDED, TILE), BF16),
            pltpu.VMEM((PADDED, TILE), BF16),
            pltpu.VMEM((NOUT_PIX, TILE), BF16),
            pltpu.VMEM((NOUT_PIX, TILE), BF16),
            pltpu.VMEM((TILE, TILE), F32),
            pltpu.VMEM((TILE, TILE), F32),
            pltpu.VMEM((TILE, TILE), F32),
            pltpu.VMEM((NOUT_PIX, ORDER), F32),
            pltpu.SemaphoreType.DMA((2 * NSEL + 2,)),
        ],
        compiler_params=pltpu.CompilerParams(vmem_limit_bytes=60 << 20),
        name="solve_stamp",
    )(pair_list, ridge, *arrays)


def blend_kernel(n_sky, n_batch, coadd_ref, out_ref, slots, send_sem, recv_sem):
    s = lax.axis_index("sky")
    b = lax.axis_index("batch")
    up = lax.rem(s + 1, n_sky)
    down = lax.rem(s + n_sky - 1, n_sky)
    right = lax.rem(b + 1, n_batch)
    left = lax.rem(b + n_batch - 1, n_batch)
    where = ((down, b), (up, b), (s, left), (s, right))
    barrier = pltpu.get_barrier_semaphore()
    for device in where:
        pl.semaphore_signal(barrier, inc=1, device_id=device, device_id_type=MESH)
    pl.semaphore_wait(barrier, 4)
    copies = [
        pltpu.make_async_remote_copy(
            src_ref=coadd_ref, dst_ref=slots.at[n], send_sem=send_sem.at[n], recv_sem=recv_sem.at[n],
            device_id=where[n], device_id_type=MESH,
        )
        for n in range(4)
    ]
    for copy in copies:
        copy.start()
    pixel = lax.broadcasted_iota(jnp.int32, (1, NOUT_PIX), 1)
    line = pixel // SIDE
    place = pixel - line * SIDE
    edge = SIDE - FADE

    def weight(at, low, first, step, there):
        value = (first + step * (at - low)).astype(F32) / (FADE + 1.0)
        value = jnp.where((at >= low) & (at < low + FADE), value, 0.0)
        return jnp.where(there, value, 0.0)

    weights = (
        weight(place, edge, 1, 1, s < n_sky - 1),
        weight(place, 0, FADE, -1, s > 0),
        weight(line, edge, 1, 1, b < n_batch - 1),
        weight(line, 0, FADE, -1, b > 0),
    )
    shifts = (edge, -edge, edge * SIDE, -edge * SIDE)
    result = coadd_ref[...]
    for n in range(4):
        copies[n].wait_recv()
        other = slots[n]
        shift = shifts[n] % NOUT_PIX
        moved = jnp.concatenate([other[:, NOUT_PIX - shift :], other[:, : NOUT_PIX - shift]], axis=1)
        result = result + weights[n] * moved
    out_ref[...] = result
    for copy in copies:
        copy.wait_send()


def blend(coadd):
    n_sky, n_batch = lax.axis_size("sky"), lax.axis_size("batch")
    return pl.pallas_call(
        functools.partial(blend_kernel, n_sky, n_batch),
        out_shape=jax.ShapeDtypeStruct((LAYERS, NOUT_PIX), F32),
        in_specs=[pl.BlockSpec(memory_space=pltpu.VMEM)],
        out_specs=pl.BlockSpec(memory_space=pltpu.VMEM),
        scratch_shapes=[
            pltpu.VMEM((4, LAYERS, NOUT_PIX), F32),
            pltpu.SemaphoreType.DMA((4,)),
            pltpu.SemaphoreType.DMA((4,)),
        ],
        compiler_params=pltpu.CompilerParams(collective_id=1, has_side_effects=True, vmem_limit_bytes=4 << 20),
        name="blend_edges",
    )(coadd)


def local(features, target, images, layer_mask, pair_list, ridge_weight):
    gathered = gather_window(
        features.reshape(NPIX, FEAT),
        images.reshape(LAYERS, NPIX),
        layer_mask.reshape(LAYERS),
        target.reshape(NOUT_PIX, FEAT),
    )
    transfer, coadd = solve(pair_list.reshape(NSEL), ridge_weight.reshape(1), *gathered)
    final = blend(coadd)
    return (transfer.T.reshape(1, 1, ORDER, NOUT_PIX), final.reshape(LAYERS, SIDE, SIDE))


def solution(mesh):
    in_specs = (
        P("batch", "sky", None, None),
        P("batch", "sky", None, None),
        P("batch", "sky", None, None),
        P("batch", "sky", None),
        P("batch", "sky", None),
        P("batch", "sky"),
    )
    out_specs = (P("batch", "sky", None, None), P(None, "batch", "sky"))
    return jax.shard_map(local, mesh=mesh, in_specs=in_specs, out_specs=out_specs, check_vma=False)
```
